32 devices in a mesh: group: 2 (over core), gx: 4 (over y, x), gy: 4 (over z).
Axes of the slice: x: 2, y: 2, z: 4, core: 2. Of those that a mesh axis runs over, the one named last changes fastest.
Arguments:
- start_vectors: float32 [2, 4, 4, 8, 384, 128], P('group', 'gx', 'gy')
- tile_blocks: bfloat16 [2, 4, 4, 8, 4, 384, 384], P('group', 'gx', 'gy')
- block_columns: int32 [2, 4, 4, 8, 4], P('group', 'gx', 'gy'), may hold values from 0 to 11, as said below
- sleeve_rod: int32 [4, 4, 1, 4, 8], P('gx', 'gy'), may hold values from -1 to 511, as said below
- sleeve_membrane: int32 [4, 4, 1, 4, 8], P('gx', None, None, 'gy'), may hold values from -1 to 511, as said below
- sleeve_stiffness: float32 [4, 4, 1, 4, 8], P('gx', None, None, 'gy'), may hold values from 0.25 to 4
Outputs:
- final_vectors: float32 [2, 4, 4, 8, 384, 128], P('group', 'gx', 'gy')
- norms: float32 [3, 128], replicated
The draws below stay inside these ranges and needn't reach their ends.
Inputs may be any that keep to these rules, and one draw needn't show every extreme that they name: `block_columns`: entry 0 of block row r is r itself; every other entry names one of the device's 8 blocks, or 8 to 11 for the west, east, south and north ghost blocks. sleeve_rod[x, y, m, y2, :] lists the nodes of rod device (0, x, y) tied to membrane tile (m + 1, x, y2); -1 marks an empty slot and live slots come first. In every draw one membrane tile receives 8 live slots from each of the 4 rod devices of its column. `sleeve_membrane`: -1 at exactly the slots where sleeve_rod is -1; elsewhere a node of membrane tile (m + 1, x, y2).
All inputs are finite; a program needn't handle non-finite values.
Results may differ from the reference program's by a relative error of at most 0.005.
Values may be sent and summed in bfloat16 or wider, within the bound.
A program may use at most 64 MiB of HBM per device.

```python
import math
import jax
import jax.numpy as jnp
from jax import lax

TILE = 384
NB = 8
KB = 4
S = 128
CAP = 8
MATVECS = 3
MEMB = 1
NODES_DEV = 512
N_GROUP = 2
N_GX = 4
N_GY = 4


def device_ramp():
    position = (jnp.arange(N_GROUP)[:, None, None] * N_GX + jnp.arange(N_GX)[None, :, None]) * N_GY + jnp.arange(N_GY)[None, None, :]
    return jnp.exp(math.log(3.0) * position.astype(jnp.float32) / max(N_GROUP * N_GX * N_GY - 1, 1))


def draw_start_vectors(key, part):
    first, second = jax.random.split(jax.random.fold_in(key, 3))
    shape = (N_GROUP, N_GX, N_GY, NB, TILE, S)
    noise = jax.random.normal(first, shape, jnp.float32)
    column = jnp.exp(jax.random.uniform(second, (S,), jnp.float32, math.log(0.3), math.log(3.0)))
    return noise * column * device_ramp()[:, :, :, None, None, None]


def draw_tile_blocks(key, part):
    first, second = jax.random.split(jax.random.fold_in(key, 13))
    shape = (N_GROUP, N_GX, N_GY, NB, KB, TILE, TILE)
    noise = jax.random.normal(first, shape, jnp.float32)
    row_scale = jnp.exp(jax.random.uniform(second, (N_GROUP, N_GX, N_GY, NB, 1, TILE, 1), jnp.float32, math.log(0.4), math.log(4.0)))
    ramp = device_ramp()[:, :, :, None, None, None, None]
    return (noise * row_scale * ramp / math.sqrt(KB * TILE)).astype(jnp.bfloat16)


def draw_block_columns(key, part):
    shape = (N_GROUP, N_GX, N_GY, NB, KB)
    extra = jax.random.randint(jax.random.fold_in(key, 11), shape, 0, NB + 4, dtype=jnp.int32)
    own_row = jnp.broadcast_to(jnp.arange(NB, dtype=jnp.int32)[:, None], (NB, KB))
    slot_first = jnp.arange(KB)[None, :] == 0
    return jnp.where(slot_first, own_row, extra).astype(jnp.int32)


def sleeve_lists(key):
    keys = jax.random.split(jax.random.fold_in(key, 29), 8)
    shape = (N_GX, N_GY, MEMB, N_GY)
    base = jax.random.randint(keys[0], shape, 1, max(CAP // 4, 1) + 1, dtype=jnp.int32)
    hot_rows = jax.random.randint(keys[1], (N_GX, N_GY, 1, 1), 0, 4, dtype=jnp.int32) == 0
    heavy = jax.random.randint(keys[2], shape, max(CAP // 2, 1), CAP + 1, dtype=jnp.int32)
    counts = jnp.where(hot_rows, heavy, base)
    full_x = jax.random.randint(keys[3], (), 0, N_GX, dtype=jnp.int32)
    full_m = jax.random.randint(keys[4], (), 0, MEMB, dtype=jnp.int32)
    full_y = jax.random.randint(keys[5], (), 0, N_GY, dtype=jnp.int32)
    forced = (jnp.arange(N_GX)[:, None, None, None] == full_x) & (jnp.arange(MEMB)[None, None, :, None] == full_m) & (jnp.arange(N_GY)[None, None, None, :] == full_y)
    counts = jnp.where(forced, CAP, counts)
    live = jnp.arange(CAP)[None, None, None, None, :] < counts[..., None]
    rod_nodes = jax.random.randint(keys[6], shape + (CAP,), 0, NODES_DEV, dtype=jnp.int32)
    memb_nodes = jax.random.randint(keys[7], shape + (CAP,), 0, NODES_DEV, dtype=jnp.int32)
    return (jnp.where(live, rod_nodes, -1).astype(jnp.int32), jnp.where(live, memb_nodes, -1).astype(jnp.int32))


def draw_sleeve_rod(key, part):
    return sleeve_lists(key)[0]


def draw_sleeve_membrane(key, part):
    return sleeve_lists(key)[1]


def levels(key, shape, cuts, smallest, top_value):
    def one(dim, parts):
        draws = jax.random.uniform(jax.random.fold_in(jax.random.fold_in(key, 6), dim), (parts,), jnp.float32, smallest / len(cuts), top_value / len(cuts))
        return jnp.repeat(jnp.exp(draws), shape[dim] // parts).reshape((-1,) + (1,) * (len(shape) - dim - 1))

    gain = one(*cuts[0])
    for cut in cuts[1:]:
        gain = gain * one(*cut)
    return gain


def setup_inputs(seed: int = 0) -> dict:
    arg_keys = jax.random.split(jax.random.key(seed), 7)
    start_vectors = draw_start_vectors(jax.random.fold_in(arg_keys[6], 71), 0)
    tile_blocks = draw_tile_blocks(jax.random.fold_in(arg_keys[6], 71), 0)
    block_columns = draw_block_columns(jax.random.fold_in(arg_keys[6], 71), 0)
    sleeve_rod = draw_sleeve_rod(jax.random.fold_in(arg_keys[6], 71), 0)
    sleeve_membrane = draw_sleeve_membrane(jax.random.fold_in(arg_keys[6], 71), 0)
    sleeve_stiffness = jnp.clip(jnp.exp(math.log(4.0) - 2.7725887 * jax.random.uniform(arg_keys[5], (N_GX, N_GY, MEMB, N_GY, CAP), jnp.float32) ** levels(arg_keys[5], (N_GX, N_GY, MEMB, N_GY, CAP), ((0, 4), (3, 4)), -0.2, 0.2)), 0.25, 4.0)
    return dict(start_vectors=start_vectors, tile_blocks=tile_blocks, block_columns=block_columns, sleeve_rod=sleeve_rod, sleeve_membrane=sleeve_membrane, sleeve_stiffness=sleeve_stiffness)


def reference(start_vectors, tile_blocks, block_columns, sleeve_rod, sleeve_membrane, sleeve_stiffness):
    devices_all = N_GROUP * N_GX * N_GY
    nodes = NB * TILE // 6
    payload = 6 * S
    blocks = tile_blocks.reshape(devices_all, NB, KB, TILE, TILE)
    columns = block_columns.reshape(devices_all, NB * KB)
    live = sleeve_rod >= 0
    rod_safe = jnp.maximum(sleeve_rod, 0)
    memb_safe = jnp.maximum(sleeve_membrane, 0)
    stiffs = jnp.where(live, sleeve_stiffness, jnp.float32(0.0))
    shape5 = sleeve_rod.shape
    x_index = jnp.broadcast_to(jnp.arange(N_GX, dtype=jnp.int32)[:, None, None, None, None], shape5)
    y_source = jnp.broadcast_to(jnp.arange(N_GY, dtype=jnp.int32)[None, :, None, None, None], shape5)
    m_index = jnp.broadcast_to(jnp.arange(MEMB, dtype=jnp.int32)[None, None, :, None, None], shape5) + 1
    y_target = jnp.broadcast_to(jnp.arange(N_GY, dtype=jnp.int32)[None, None, None, :, None], shape5)
    g_zero = jnp.zeros(shape5, jnp.int32)

    def one_device(args):
        local_blocks, local_ext, local_cols = args
        picked = jnp.take(local_ext, local_cols, axis=0).reshape(NB, KB, TILE, S)
        return jnp.einsum('rkij,rkjs->ris', local_blocks.astype(jnp.float32), picked.astype(jnp.float32), precision=lax.Precision.HIGHEST)
    current = start_vectors
    norms = []
    for matvec in range(MATVECS):
        rounded = current.astype(jnp.bfloat16)
        zero_x = jnp.zeros_like(rounded[:, :1, :, 0])
        west = jnp.concatenate([zero_x, rounded[:, :-1, :, NB - 1]], axis=1)
        east = jnp.concatenate([rounded[:, 1:, :, 0], zero_x], axis=1)
        zero_y = jnp.zeros_like(rounded[:, :, :1, 0])
        south = jnp.concatenate([zero_y, rounded[:, :, :-1, 1]], axis=2)
        north = jnp.concatenate([rounded[:, :, 1:, NB - 2], zero_y], axis=2)
        extended = jnp.concatenate([rounded, west[:, :, :, None], east[:, :, :, None], south[:, :, :, None], north[:, :, :, None]], axis=3)
        extended = extended.reshape(devices_all, NB + 4, TILE, S)
        product = lax.map(one_device, (blocks, extended, columns)).reshape(N_GROUP, N_GX, N_GY, NB, TILE, S)
        node_rows = rounded.reshape(N_GROUP, N_GX, N_GY, nodes, payload).astype(jnp.float32)
        rod_values = node_rows[0][x_index, y_source, rod_safe]
        memb_values = node_rows[m_index, x_index, y_target, memb_safe]
        delta = stiffs[..., None] * (memb_values - rod_values)
        reaction = delta.astype(jnp.bfloat16).astype(jnp.float32)
        coupling = jnp.zeros_like(node_rows).at[m_index, x_index, y_target, memb_safe].add(delta)
        coupling = coupling.at[g_zero, x_index, y_source, rod_safe].add(-reaction)
        coupled = product + coupling.reshape(product.shape)
        squares = lax.optimization_barrier(jnp.sum(coupled * coupled, axis=(0, 1, 2, 3, 4)))
        scale = jnp.sqrt(squares / (devices_all * NB * TILE) + 1e-06)
        current = coupled / scale
        norms.append(scale)
    return (current, jnp.stack(norms))
```

```python
import functools

import jax
import jax.numpy as jnp
from jax import lax
from jax.experimental import pallas as pl
from jax.experimental.pallas import tpu as pltpu
from jax.sharding import PartitionSpec as P

MATVECS = 3
DOFS = 6
EPSILON = 1e-06
MESH = pl.DeviceIdType.MESH
F32 = jnp.float32
BF16 = jnp.bfloat16


def kernel(groups, gxs, gys, nb, kb, width, lanes, rows,
           cols, idx_col, idx_row, kap_col, v_hbm, a_hbm,
           out_hbm, norms,
           a, ext_0, ext_1, ext_2, v32, acc0, c3, gat, sca, own, oth, kown, kap, dlt, sqacc, sqa, sqb, inv,
           v_sem, a0_sem, a_sem, o_sem, gs, gr, ss, sr, ks, kr, as_, ar, bs, br):
    ext = (ext_0, ext_1, ext_2)
    g = lax.axis_index("group")
    x = lax.axis_index("gx")
    y = lax.axis_index("gy")
    plane = g * gxs + x
    rod = g == 0
    members = groups - 1
    chunks = members * gys
    all_dofs = float(groups * gxs * gys * nb * width)

    def row_of(i):
        half, odd = lax.div(i, 2), lax.rem(i, 2)
        return half * (1 - 2 * odd) + odd * (nb - 1)

    order = [i // 2 if i % 2 == 0 else nb - 1 - i // 2 for i in range(nb)]
    for r in order:
        pltpu.make_async_copy(v_hbm.at[r], v32.at[r], v_sem.at[r]).start()
    pltpu.make_async_copy(a_hbm.at[:, 0], a.at[:, 0], a0_sem).start()
    for r in order:
        pltpu.make_async_copy(a_hbm.at[r, pl.ds(1, kb - 1)], a.at[r, pl.ds(1, kb - 1)], a_sem.at[r]).start()

    barrier = pltpu.get_barrier_semaphore()
    for i in range(gys):
        @pl.when(i != y)
        def _():
            pl.semaphore_signal(barrier, inc=1, device_id=(g, x, i), device_id_type=MESH)
    for p in range(groups * gxs):
        @pl.when(p != plane)
        def _():
            pl.semaphore_signal(barrier, inc=1, device_id=(p // gxs, p % gxs, y), device_id_type=MESH)

    def peer(c):
        return (jnp.where(rod, c // gys + 1, 0), x, c % gys)

    def each_chunk(body):
        for c in range(chunks):
            if c < gys:
                body(c)
            else:
                pl.when(rod)(functools.partial(body, c))

    each_chunk(lambda c: pl.semaphore_signal(barrier, inc=1, device_id=peer(c), device_id_type=MESH))

    sides = (
        (nb - 1, x < gxs - 1, lambda: (g, x + 1, y), x > 0, lambda: (g, x - 1, y)),
        (0, x > 0, lambda: (g, x - 1, y), x < gxs - 1, lambda: (g, x + 1, y)),
        (1, y < gys - 1, lambda: (g, x, y + 1), y > 0, lambda: (g, x, y - 1)),
        (nb - 2, y > 0, lambda: (g, x, y - 1), y < gys - 1, lambda: (g, x, y + 1)),
    )
    for d, (_, _, _, hears, _) in enumerate(sides):
        @pl.when(jnp.logical_not(hears))
        def _():
            for s in range(MATVECS):
                ext[s][nb + d] = jnp.zeros((width, lanes), BF16)

    kown[...] = jnp.broadcast_to(kap_col[...], (gys * rows, lanes)).reshape(gys, rows, lanes)

    @pl.when(jnp.logical_not(rod))
    def _():
        kap[0] = kown[...]
        for m in range(1, members):
            kap[m] = jnp.zeros((gys, rows, lanes), F32)
            for s in range(MATVECS):
                oth[s, m] = jnp.zeros((gys, rows, lanes), BF16)

    def gather_matrix(m, carry):
        for r in range(nb):
            dof = lax.broadcasted_iota(jnp.int32, (gys * rows, width), 1) + r * width
            hot = jnp.where(idx_col[m] == dof, F32(1.0), F32(0.0)).astype(BF16)
            gat[m, :, r * width:(r + 1) * width] = hot
        return carry

    lax.fori_loop(0, members, gather_matrix, 0)

    for r in order[:4]:
        pltpu.make_async_copy(v_hbm.at[r], v32.at[r], v_sem.at[r]).wait()
        ext[0][r] = v32[r].astype(BF16)

    pl.semaphore_wait(barrier, gys - 1 + groups * gxs - 1 + jnp.where(rod, chunks, gys))

    def side_copy(s, d, device):
        return pltpu.make_async_remote_copy(
            src_ref=ext[s].at[sides[d][0]], dst_ref=ext[s].at[nb + d],
            send_sem=gs.at[s, d], recv_sem=gr.at[s, d],
            device_id=device, device_id_type=MESH)

    def send_sides(s):
        for d, (_, sends, to, _, _) in enumerate(sides):
            @pl.when(sends)
            def _():
                side_copy(s, d, to()).start()

    def wait_sides(s):
        for d, (_, _, _, hears, source) in enumerate(sides):
            @pl.when(hears)
            def _():
                side_copy(s, d, source()).wait_recv()

    my_chunk = jnp.where(rod, y, (g - 1) * gys + y)

    def sleeve_copy(s, c, dst):
        return pltpu.make_async_remote_copy(
            src_ref=own.at[s, c // gys, c % gys], dst_ref=oth.at[s, dst // gys, dst % gys],
            send_sem=ss.at[s, c], recv_sem=sr.at[s, dst],
            device_id=peer(c), device_id_type=MESH)

    def kap_copy(c, dst):
        return pltpu.make_async_remote_copy(
            src_ref=kown.at[c % gys], dst_ref=kap.at[dst // gys, dst % gys],
            send_sem=ks.at[c % gys], recv_sem=kr.at[dst],
            device_id=peer(c), device_id_type=MESH)

    send_sides(0)

    @pl.when(jnp.logical_not(rod))
    def _():
        for c in range(gys):
            kap_copy(c, my_chunk).start()

    for r in order[4:]:
        pltpu.make_async_copy(v_hbm.at[r], v32.at[r], v_sem.at[r]).wait()
        ext[0][r] = v32[r].astype(BF16)

    def gather(s):
        def one(m, carry):
            got = jnp.dot(gat[m], ext[s][:nb].reshape(nb * width, lanes), preferred_element_type=F32)
            own[s, m] = got.astype(BF16).reshape(gys, rows, lanes)
            return carry

        lax.fori_loop(0, members, one, 0)
        each_chunk(lambda c: sleeve_copy(s, c, my_chunk).start())

    def first_blocks(s):
        def one(r, carry):
            acc0[r] = jnp.dot(a[r, 0], ext[s][r], preferred_element_type=F32)
            return carry

        lax.fori_loop(0, nb, one, 0)

    def spring_forces(s):
        each_chunk(lambda c: sleeve_copy(s, c, c).wait_recv())
        for m in range(members):
            force = kap[m] * (own[s, m].astype(F32) - oth[s, m].astype(F32))
            dlt[m * gys * rows:(m + 1) * gys * rows] = force.astype(BF16).reshape(gys * rows, lanes)

    def main_rows(s, start, stop):
        def one(i, carry):
            r = row_of(i)
            if s == 0:
                pltpu.make_async_copy(
                    a_hbm.at[r, pl.ds(1, kb - 1)], a.at[r, pl.ds(1, kb - 1)], a_sem.at[r]).wait()
            left = jnp.concatenate([a[r, k] for k in range(1, kb)] + [sca[r]], axis=1)
            right = jnp.concatenate([ext[s][cols[r * kb + k]] for k in range(1, kb)] + [dlt[...]], axis=0)
            c = acc0[r] + jnp.dot(left, right, preferred_element_type=F32)
            if s > 0:
                c = c * inv[...]
            sqacc[...] += jnp.sum((c * c).reshape(width // 8, 8, lanes), axis=0)
            if s < MATVECS - 1:
                ext[s + 1][r] = c.astype(BF16)
            else:
                c3[r] = c
                pltpu.make_async_copy(c3.at[r], out_hbm.at[r], o_sem.at[r]).start()
            return carry

        lax.fori_loop(start, stop, one, 0)

    def line_copy(s, i, slot):
        return pltpu.make_async_remote_copy(
            src_ref=sqa.at[s, y], dst_ref=sqa.at[s, slot],
            send_sem=as_.at[s, i], recv_sem=ar.at[s, slot],
            device_id=(g, x, i), device_id_type=MESH)

    def plane_copy(s, p, slot):
        return pltpu.make_async_remote_copy(
            src_ref=sqb.at[s, plane], dst_ref=sqb.at[s, slot],
            send_sem=bs.at[s, p], recv_sem=br.at[s, slot],
            device_id=(p // gxs, p % gxs, y), device_id_type=MESH)

    def squares_line(s):
        sqa[s, y] = sqacc[...]
        for i in range(gys):
            @pl.when(i != y)
            def _():
                line_copy(s, i, y).start()

    def squares_plane(s):
        for i in range(gys):
            @pl.when(i != y)
            def _():
                line_copy(s, i, i).wait_recv()
        total = sqa[s, 0]
        for i in range(1, gys):
            total = total + sqa[s, i]
        sqb[s, plane] = total
        for p in range(groups * gxs):
            @pl.when(p != plane)
            def _():
                plane_copy(s, p, plane).start()

    def squares_end(s):
        for p in range(groups * gxs):
            @pl.when(p != plane)
            def _():
                plane_copy(s, p, p).wait_recv()
        total = sqb[s, 0]
        for p in range(1, groups * gxs):
            total = total + sqb[s, p]
        scale = jnp.sqrt(jnp.sum(total, axis=0, keepdims=True) / all_dofs + EPSILON)
        norms[s:s + 1, :] = scale
        inv[...] = 1.0 / scale

    for s in range(MATVECS):
        gather(s)
        if s == 0:
            def scatter_matrix(r, carry):
                dof = lax.broadcasted_iota(jnp.int32, (width, sca.shape[2]), 0) + r * width
                sca[r] = jnp.where(idx_row[...] == dof, F32(1.0), F32(0.0)).astype(BF16)
                return carry

            lax.fori_loop(0, nb, scatter_matrix, 0)
            if dlt.shape[0] > chunks * rows:
                dlt[chunks * rows:] = jnp.zeros((dlt.shape[0] - chunks * rows, lanes), BF16)
            pltpu.make_async_copy(a_hbm.at[:, 0], a.at[:, 0], a0_sem).wait()
        first_blocks(s)
        if s > 0:
            squares_plane(s - 1)
        else:
            @pl.when(rod)
            def _():
                for c in range(chunks):
                    kap_copy(c, c).wait_recv()
        spring_forces(s)
        wait_sides(s)
        if s > 0:
            squares_end(s - 1)
        sqacc[...] = jnp.zeros_like(sqacc)
        main_rows(s, 0, 4)
        if s < MATVECS - 1:
            send_sides(s + 1)
        main_rows(s, 4, nb)
        squares_line(s)
    squares_plane(MATVECS - 1)
    for s in range(MATVECS):
        for d, (_, sends, to, _, _) in enumerate(sides):
            @pl.when(sends)
            def _():
                side_copy(s, d, to()).wait_send()
        each_chunk(lambda c: sleeve_copy(s, c, c).wait_send())
        for i in range(gys):
            @pl.when(i != y)
            def _():
                line_copy(s, i, y).wait_send()

    @pl.when(jnp.logical_not(rod))
    def _():
        for c in range(gys):
            kap_copy(c, c).wait_send()

    for r in range(nb):
        pltpu.make_async_copy(c3.at[r], out_hbm.at[r], o_sem.at[r]).wait()
    squares_end(MATVECS - 1)
    for s in range(MATVECS):
        for p in range(groups * gxs):
            @pl.when(p != plane)
            def _():
                plane_copy(s, p, plane).wait_send()


def local(groups, gxs, gys, start_vectors, tile_blocks, block_columns, sleeve_rod, sleeve_membrane, sleeve_stiffness):
    nb, kb, width = tile_blocks.shape[3:6]
    lanes = start_vectors.shape[5]
    cap = sleeve_rod.shape[4]
    members = groups - 1
    rows = cap * DOFS
    chunks = members * gys
    slot_rows = chunks * rows
    padded = -(-slot_rows // 256) * 256
    g = lax.axis_index("group")
    member = jnp.maximum(g - 1, 0)
    memb = lax.dynamic_index_in_dim(sleeve_membrane[0, :, :, 0, :], member, axis=1, keepdims=False).reshape(-1)
    stiff = lax.dynamic_index_in_dim(sleeve_stiffness[0, :, :, 0, :], member, axis=1, keepdims=False).reshape(-1)
    memb = jnp.pad(memb, (0, (members - 1) * gys * cap), constant_values=-1)
    nodes = jnp.where(g == 0, sleeve_rod[0, 0].reshape(-1), memb)
    index = jnp.where(nodes[:, None] >= 0, nodes[:, None] * DOFS + jnp.arange(DOFS, dtype=jnp.int32)[None, :], -1)
    index = index.reshape(-1)
    idx_col = index.reshape(members, gys * rows, 1)
    idx_row = jnp.pad(index, (0, padded - slot_rows), constant_values=-1).reshape(1, padded)
    kap_col = jnp.broadcast_to(stiff[:, None], (gys * cap, DOFS)).reshape(gys * rows, 1)
    vmem = pl.BlockSpec(memory_space=pltpu.VMEM)
    hbm = pl.BlockSpec(memory_space=pl.ANY)
    dma = pltpu.SemaphoreType.DMA
    plane = groups * gxs
    flops = 2 * MATVECS * nb * kb * width * width * lanes
    coupled, norms = pl.pallas_call(
        functools.partial(kernel, groups, gxs, gys, nb, kb, width, lanes, rows),
        out_shape=(
            jax.ShapeDtypeStruct((nb, width, lanes), F32),
            jax.ShapeDtypeStruct((MATVECS, lanes), F32),
        ),
        in_specs=[pl.BlockSpec(memory_space=pltpu.SMEM), vmem, vmem, vmem, hbm, hbm],
        out_specs=(hbm, vmem),
        scratch_shapes=[
            pltpu.VMEM((nb, kb, width, width), BF16),
            *[pltpu.VMEM((nb + 4, width, lanes), BF16)] * MATVECS,
            pltpu.VMEM((nb, width, lanes), F32),
            pltpu.VMEM((nb, width, lanes), F32),
            pltpu.VMEM((nb, width, lanes), F32),
            pltpu.VMEM((members, gys * rows, nb * width), BF16),
            pltpu.VMEM((nb, width, padded), BF16),
            pltpu.VMEM((MATVECS, members, gys, rows, lanes), BF16),
            pltpu.VMEM((MATVECS, members, gys, rows, lanes), BF16),
            pltpu.VMEM((gys, rows, lanes), F32),
            pltpu.VMEM((members, gys, rows, lanes), F32),
            pltpu.VMEM((padded, lanes), BF16),
            pltpu.VMEM((8, lanes), F32),
            pltpu.VMEM((MATVECS, gys, 8, lanes), F32),
            pltpu.VMEM((MATVECS, plane, 8, lanes), F32),
            pltpu.VMEM((1, lanes), F32),
            dma((nb,)), dma, dma((nb,)), dma((nb,)),
            dma((MATVECS, 4)), dma((MATVECS, 4)),
            dma((MATVECS, chunks)), dma((MATVECS, chunks)),
            dma((gys,)), dma((chunks,)),
            dma((MATVECS, gys)), dma((MATVECS, gys)),
            dma((MATVECS, plane)), dma((MATVECS, plane)),
        ],
        compiler_params=pltpu.CompilerParams(
            collective_id=0, has_side_effects=True, vmem_limit_bytes=60 * 2**20),
        cost_estimate=pl.CostEstimate(flops=flops, bytes_accessed=tile_blocks.size * 2, transcendentals=0),
    )(block_columns.reshape(-1), idx_col, idx_row, kap_col,
      start_vectors.reshape(nb, width, lanes), tile_blocks.reshape(nb, kb, width, width))
    final = coupled / norms[MATVECS - 1]
    return (final[None, None, None], norms)


def solution(mesh):
    return jax.shard_map(
        functools.partial(local, mesh.shape["group"], mesh.shape["gx"], mesh.shape["gy"]),
        mesh=mesh,
        in_specs=(
            P("group", "gx", "gy", None, None, None),
            P("group", "gx", "gy", None, None, None, None),
            P("group", "gx", "gy", None, None),
            P("gx", "gy", None, None, None),
            P("gx", None, None, "gy", None),
            P("gx", None, None, "gy", None),
        ),
        out_specs=(P("group", "gx", "gy", None, None, None), P()),
        check_vma=False,
    )
```

```python
import functools

import jax
import jax.numpy as jnp
from jax import lax
from jax.experimental import pallas as pl
from jax.experimental.pallas import tpu as pltpu
from jax.sharding import PartitionSpec as P

MATVECS = 3
DOFS = 6
EPSILON = 1e-06
MESH = pl.DeviceIdType.MESH
F32 = jnp.float32
BF16 = jnp.bfloat16


def kernel(groups, gxs, gys, nb, kb, width, lanes, rows,
           cols, rod_nodes, memb_nodes, stiff, v_hbm, a_hbm,
           c3, norms, inverse,
           a, ext_0, ext_1, ext_2, acc0, gat, sca, own, oth, kown, kap, dlt, sqacc, sqa, sqb, inv,
           v_sem, a0_sem, a_sem, gs, gr, ss, sr, ks, kr, as_, ar, bs, br):
    ext = (ext_0, ext_1, ext_2)
    g = lax.axis_index("group")
    x = lax.axis_index("gx")
    y = lax.axis_index("gy")
    plane = g * gxs + x
    rod = g == 0
    members = groups - 1
    chunks = members * gys
    all_dofs = float(groups * gxs * gys * nb * width)

    def row_of(i):
        half, odd = lax.div(i, 2), lax.rem(i, 2)
        return half * (1 - 2 * odd) + odd * (nb - 1)

    order = [i // 2 if i % 2 == 0 else nb - 1 - i // 2 for i in range(nb)]
    for r in order:
        pltpu.make_async_copy(v_hbm.at[r], acc0.at[r], v_sem.at[r]).start()
    pltpu.make_async_copy(a_hbm.at[:, 0], a.at[:, 0], a0_sem).start()
    for r in order:
        pltpu.make_async_copy(a_hbm.at[r, pl.ds(1, kb - 1)], a.at[r, pl.ds(1, kb - 1)], a_sem.at[r]).start()

    barrier = pltpu.get_barrier_semaphore()
    for i in range(gys):
        @pl.when(i != y)
        def _():
            pl.semaphore_signal(barrier, inc=1, device_id=(g, x, i), device_id_type=MESH)
    for p in range(groups * gxs):
        @pl.when(p != plane)
        def _():
            pl.semaphore_signal(barrier, inc=1, device_id=(p // gxs, p % gxs, y), device_id_type=MESH)

    def peer(c):
        return (jnp.where(rod, c // gys + 1, 0), x, c % gys)

    def each_chunk(body):
        for c in range(chunks):
            if c < gys:
                body(c)
            else:
                pl.when(rod)(functools.partial(body, c))

    each_chunk(lambda c: pl.semaphore_signal(barrier, inc=1, device_id=peer(c), device_id_type=MESH))

    sides = (
        (nb - 1, x < gxs - 1, lambda: (g, x + 1, y), x > 0, lambda: (g, x - 1, y)),
        (0, x > 0, lambda: (g, x - 1, y), x < gxs - 1, lambda: (g, x + 1, y)),
        (1, y < gys - 1, lambda: (g, x, y + 1), y > 0, lambda: (g, x, y - 1)),
        (nb - 2, y > 0, lambda: (g, x, y - 1), y < gys - 1, lambda: (g, x, y + 1)),
    )
    for d, (_, _, _, hears, _) in enumerate(sides):
        @pl.when(jnp.logical_not(hears))
        def _():
            for s in range(MATVECS):
                ext[s][nb + d] = jnp.zeros((width, lanes), BF16)

    cap = rows // DOFS
    member = jnp.maximum(g - 1, 0)
    slot = lax.broadcasted_iota(jnp.int32, (cap, lanes), 0)
    for c in range(gys):
        value = jnp.zeros((cap, lanes), F32)
        for t in range(cap):
            value = jnp.where(slot == t, stiff[c, member, 0, t], value)
        for d in range(DOFS):
            kown[c, d * cap:(d + 1) * cap] = value

    @pl.when(jnp.logical_not(rod))
    def _():
        kap[0] = kown[...]
        for m in range(1, members):
            kap[m] = jnp.zeros((gys, rows, lanes), F32)
            for s in range(MATVECS):
                oth[s, m] = jnp.zeros((gys, rows, lanes), BF16)

    def node_of(m, c, t):
        return jnp.where(rod, rod_nodes[m, c, t], jnp.where(m == 0, memb_nodes[c, member, 0, t], -1))

    def gather_matrix(m, carry):
        for c in range(gys):
            value = jnp.zeros((cap, lanes), jnp.int32)
            for t in range(cap):
                value = jnp.where(slot == t, node_of(m, c, t), value)
            wanted = jnp.concatenate(
                [jnp.where(value >= 0, value * DOFS + d, -1) for d in range(DOFS)], axis=0)
            lane = lax.broadcasted_iota(jnp.int32, (rows, lanes), 1)
            for b in range(nb * width // lanes):
                hot = jnp.where(wanted == lane + b * lanes, F32(1.0), F32(0.0)).astype(BF16)
                gat[m, c * rows:(c + 1) * rows, b * lanes:(b + 1) * lanes] = hot
        return carry

    lax.fori_loop(0, members, gather_matrix, 0)

    for r in order[:4]:
        pltpu.make_async_copy(v_hbm.at[r], acc0.at[r], v_sem.at[r]).wait()
        ext[0][r] = acc0[r].astype(BF16)

    pl.semaphore_wait(barrier, gys - 1 + groups * gxs - 1 + jnp.where(rod, chunks, gys))

    def side_copy(s, d, device):
        return pltpu.make_async_remote_copy(
            src_ref=ext[s].at[sides[d][0]], dst_ref=ext[s].at[nb + d],
            send_sem=gs.at[s, d], recv_sem=gr.at[s, d],
            device_id=device, device_id_type=MESH)

    def send_sides(s):
        for d, (_, sends, to, _, _) in enumerate(sides):
            @pl.when(sends)
            def _():
                side_copy(s, d, to()).start()

    def wait_sides(s):
        for d, (_, _, _, hears, source) in enumerate(sides):
            @pl.when(hears)
            def _():
                side_copy(s, d, source()).wait_recv()

    my_chunk = jnp.where(rod, y, (g - 1) * gys + y)

    def sleeve_copy(s, c, dst):
        return pltpu.make_async_remote_copy(
            src_ref=own.at[s, c // gys, c % gys], dst_ref=oth.at[s, dst // gys, dst % gys],
            send_sem=ss.at[s, c], recv_sem=sr.at[s, dst],
            device_id=peer(c), device_id_type=MESH)

    def kap_copy(c, dst):
        return pltpu.make_async_remote_copy(
            src_ref=kown.at[c % gys], dst_ref=kap.at[dst // gys, dst % gys],
            send_sem=ks.at[c % gys], recv_sem=kr.at[dst],
            device_id=peer(c), device_id_type=MESH)

    send_sides(0)

    @pl.when(jnp.logical_not(rod))
    def _():
        for c in range(gys):
            kap_copy(c, my_chunk).start()

    for r in order[4:]:
        pltpu.make_async_copy(v_hbm.at[r], acc0.at[r], v_sem.at[r]).wait()
        ext[0][r] = acc0[r].astype(BF16)

    def gather(s):
        def one(m, carry):
            got = jnp.dot(gat[m], ext[s][:nb].reshape(nb * width, lanes), preferred_element_type=F32)
            own[s, m] = got.astype(BF16).reshape(gys, rows, lanes)
            return carry

        lax.fori_loop(0, members, one, 0)
        each_chunk(lambda c: sleeve_copy(s, c, my_chunk).start())

    def first_blocks(s):
        def one(r, carry):
            acc0[r] = jnp.dot(a[r, 0], ext[s][r], preferred_element_type=F32)
            return carry

        lax.fori_loop(0, nb, one, 0, unroll=4)

    def spring_forces(s):
        each_chunk(lambda c: sleeve_copy(s, c, c).wait_recv())
        for m in range(members):
            force = kap[m] * (own[s, m].astype(F32) - oth[s, m].astype(F32))
            dlt[m * gys * rows:(m + 1) * gys * rows] = force.astype(BF16).reshape(gys * rows, lanes)

    def main_rows(s, start, stop):
        def one(i, carry):
            r = row_of(i)
            if s == 0:
                pltpu.make_async_copy(
                    a_hbm.at[r, pl.ds(1, kb - 1)], a.at[r, pl.ds(1, kb - 1)], a_sem.at[r]).wait()
            left = jnp.concatenate([a[r, k] for k in range(1, kb)] + [sca[r]], axis=1)
            right = jnp.concatenate([ext[s][cols[k, r]] for k in range(1, kb)] + [dlt[...]], axis=0)
            c = acc0[r] + jnp.dot(left, right, preferred_element_type=F32)
            if s > 0:
                c = c * inv[...]
            sqacc[...] += jnp.sum((c * c).reshape(width // 8, 8, lanes), axis=0)
            if s < MATVECS - 1:
                ext[s + 1][r] = c.astype(BF16)
            else:
                c3[r] = c
            return carry

        lax.fori_loop(start, stop, one, 0, unroll=2)

    def line_copy(s, i, slot):
        return pltpu.make_async_remote_copy(
            src_ref=sqa.at[s, y], dst_ref=sqa.at[s, slot],
            send_sem=as_.at[s, i], recv_sem=ar.at[s, slot],
            device_id=(g, x, i), device_id_type=MESH)

    def plane_copy(s, p, slot):
        return pltpu.make_async_remote_copy(
            src_ref=sqb.at[s, plane], dst_ref=sqb.at[s, slot],
            send_sem=bs.at[s, p], recv_sem=br.at[s, slot],
            device_id=(p // gxs, p % gxs, y), device_id_type=MESH)

    def squares_line(s):
        sqa[s, y] = sqacc[...]
        for i in range(gys):
            @pl.when(i != y)
            def _():
                line_copy(s, i, y).start()

    def squares_plane(s):
        for i in range(gys):
            @pl.when(i != y)
            def _():
                line_copy(s, i, i).wait_recv()
        total = sqa[s, 0]
        for i in range(1, gys):
            total = total + sqa[s, i]
        sqb[s, plane] = total
        for p in range(groups * gxs):
            @pl.when(p != plane)
            def _():
                plane_copy(s, p, plane).start()

    def squares_end(s):
        for p in range(groups * gxs):
            @pl.when(p != plane)
            def _():
                plane_copy(s, p, p).wait_recv()
        total = sqb[s, 0]
        for p in range(1, groups * gxs):
            total = total + sqb[s, p]
        scale = jnp.sqrt(jnp.sum(total, axis=0, keepdims=True) / all_dofs + EPSILON)
        norms[s:s + 1, :] = scale
        inv[...] = 1.0 / scale
        if s == MATVECS - 1:
            inverse[...] = 1.0 / scale

    for s in range(MATVECS):
        gather(s)
        if s == 0:
            padded = sca.shape[2]
            place = lax.broadcasted_iota(jnp.int32, (8, padded), 1)
            within = lax.rem(place, rows)
            key = lax.div(place, rows) * cap + lax.rem(within, cap)

            def slot_row(j, value):
                c = lax.div(j, cap)
                node = node_of(lax.div(c, gys), lax.rem(c, gys), lax.rem(j, cap))
                return jnp.where(key == j, node, value)

            node_row = lax.fori_loop(0, chunks * cap, slot_row, jnp.full((8, padded), -1, jnp.int32))
            node_row = jnp.where(node_row >= 0, node_row * DOFS + lax.div(within, cap), -1)

            def scatter_matrix(r, carry):
                dof = lax.broadcasted_iota(jnp.int32, (width, padded), 0) + r * width
                sca[r] = jnp.where(node_row[:1] == dof, F32(1.0), F32(0.0)).astype(BF16)
                return carry

            lax.fori_loop(0, nb, scatter_matrix, 0)
            if dlt.shape[0] > chunks * rows:
                dlt[chunks * rows:] = jnp.zeros((dlt.shape[0] - chunks * rows, lanes), BF16)
            pltpu.make_async_copy(a_hbm.at[:, 0], a.at[:, 0], a0_sem).wait()
        first_blocks(s)
        if s > 0:
            squares_plane(s - 1)
        else:
            @pl.when(rod)
            def _():
                for c in range(chunks):
                    kap_copy(c, c).wait_recv()
        spring_forces(s)
        wait_sides(s)
        if s > 0:
            squares_end(s - 1)
        sqacc[...] = jnp.zeros_like(sqacc)
        main_rows(s, 0, 4)
        if s < MATVECS - 1:
            send_sides(s + 1)
        main_rows(s, 4, nb)
        squares_line(s)
    squares_plane(MATVECS - 1)
    for s in range(MATVECS):
        for d, (_, sends, to, _, _) in enumerate(sides):
            @pl.when(sends)
            def _():
                side_copy(s, d, to()).wait_send()
        each_chunk(lambda c: sleeve_copy(s, c, c).wait_send())
        for i in range(gys):
            @pl.when(i != y)
            def _():
                line_copy(s, i, y).wait_send()

    @pl.when(jnp.logical_not(rod))
    def _():
        for c in range(gys):
            kap_copy(c, c).wait_send()

    squares_end(MATVECS - 1)
    for s in range(MATVECS):
        for p in range(groups * gxs):
            @pl.when(p != plane)
            def _():
                plane_copy(s, p, plane).wait_send()


def local(groups, gxs, gys, start_vectors, tile_blocks, block_columns, sleeve_rod, sleeve_membrane, sleeve_stiffness):
    nb, kb, width = tile_blocks.shape[3:6]
    lanes = start_vectors.shape[5]
    cap = sleeve_rod.shape[4]
    members = groups - 1
    rows = cap * DOFS
    chunks = members * gys
    slot_rows = chunks * rows
    padded = -(-slot_rows // 256) * 256
    smem = pl.BlockSpec(memory_space=pltpu.SMEM)
    vmem = pl.BlockSpec(memory_space=pltpu.VMEM)
    hbm = pl.BlockSpec(memory_space=pl.ANY)
    dma = pltpu.SemaphoreType.DMA
    plane = groups * gxs
    flops = 2 * MATVECS * nb * kb * width * width * lanes
    coupled, norms, inverse = pl.pallas_call(
        functools.partial(kernel, groups, gxs, gys, nb, kb, width, lanes, rows),
        out_shape=(
            pltpu.VMEM((nb, width, lanes), F32),
            jax.ShapeDtypeStruct((MATVECS, lanes), F32),
            jax.ShapeDtypeStruct((1, lanes), F32),
        ),
        in_specs=[smem, smem, smem, smem, hbm, hbm],
        out_specs=(vmem, vmem, vmem),
        scratch_shapes=[
            pltpu.VMEM((nb, kb, width, width), BF16),
            *[pltpu.VMEM((nb + 4, width, lanes), BF16)] * MATVECS,
            pltpu.VMEM((nb, width, lanes), F32),
            pltpu.VMEM((members, gys * rows, nb * width), BF16),
            pltpu.VMEM((nb, width, padded), BF16),
            pltpu.VMEM((MATVECS, members, gys, rows, lanes), BF16),
            pltpu.VMEM((MATVECS, members, gys, rows, lanes), BF16),
            pltpu.VMEM((gys, rows, lanes), F32),
            pltpu.VMEM((members, gys, rows, lanes), F32),
            pltpu.VMEM((padded, lanes), BF16),
            pltpu.VMEM((8, lanes), F32),
            pltpu.VMEM((MATVECS, gys, 8, lanes), F32),
            pltpu.VMEM((MATVECS, plane, 8, lanes), F32),
            pltpu.VMEM((1, lanes), F32),
            dma((nb,)), dma, dma((nb,)),
            dma((MATVECS, 4)), dma((MATVECS, 4)),
            dma((MATVECS, chunks)), dma((MATVECS, chunks)),
            dma((gys,)), dma((chunks,)),
            dma((MATVECS, gys)), dma((MATVECS, gys)),
            dma((MATVECS, plane)), dma((MATVECS, plane)),
        ],
        compiler_params=pltpu.CompilerParams(
            collective_id=0, has_side_effects=True, vmem_limit_bytes=58 * 2**20),
        cost_estimate=pl.CostEstimate(flops=flops, bytes_accessed=tile_blocks.size * 2, transcendentals=0),
    )(block_columns[0, 0, 0].T, sleeve_rod[0, 0], sleeve_membrane[0], sleeve_stiffness[0],
      start_vectors.reshape(nb, width, lanes), tile_blocks.reshape(nb, kb, width, width))
    final = coupled * inverse
    return (final[None, None, None], norms)


def solution(mesh):
    return jax.shard_map(
        functools.partial(local, mesh.shape["group"], mesh.shape["gx"], mesh.shape["gy"]),
        mesh=mesh,
        in_specs=(
            P("group", "gx", "gy", None, None, None),
            P("group", "gx", "gy", None, None, None, None),
            P("group", "gx", "gy", None, None),
            P("gx", "gy", None, None, None),
            P("gx", None, None, "gy", None),
            P("gx", None, None, "gy", None),
        ),
        out_specs=(P("group", "gx", "gy", None, None, None), P()),
        check_vma=False,
    )
```

```python
import functools

import jax
import jax.numpy as jnp
from jax import lax
from jax.experimental import pallas as pl
from jax.experimental.pallas import tpu as pltpu
from jax.sharding import PartitionSpec as P

MATVECS = 3
DOFS = 6
EPSILON = 1e-06
MESH = pl.DeviceIdType.MESH
F32 = jnp.float32
BF16 = jnp.bfloat16


def kernel(groups, gxs, gys, nb, kb, width, lanes, rows,
           cols_hbm, rod_hbm, memb_hbm, stiff_hbm, v_hbm, a_hbm,
           result, norms,
           cols, rod_nodes, memb_nodes, stiff, a, ext, land, acc0, gat, sca, own, oth, kown, kap, dlt, sqacc, sqa, sqb, inv,
           i_sem, v_sem, a0_sem, a_sem, gs, gr, ss, sr, ks, kr, as_, ar, bs, br):
    g = lax.axis_index("group")
    x = lax.axis_index("gx")
    y = lax.axis_index("gy")
    plane = g * gxs + x
    rod = g == 0
    members = groups - 1
    chunks = members * gys
    all_dofs = float(groups * gxs * gys * nb * width)

    def row_of(i):
        half, odd = lax.div(i, 2), lax.rem(i, 2)
        return half * (1 - 2 * odd) + odd * (nb - 1)

    order = [i // 2 if i % 2 == 0 else nb - 1 - i // 2 for i in range(nb)]
    for r in order:
        pltpu.make_async_copy(v_hbm.at[r], acc0.at[r], v_sem.at[r]).start()
    pltpu.make_async_copy(a_hbm.at[:, 0], a.at[:, 0], a0_sem).start()
    for r in order:
        pltpu.make_async_copy(a_hbm.at[r, pl.ds(1, kb - 1)], a.at[r, pl.ds(1, kb - 1)], a_sem.at[r]).start()

    small = [
        pltpu.make_async_copy(src, dst, i_sem.at[i])
        for i, (src, dst) in enumerate(
            ((rod_hbm, rod_nodes), (memb_hbm, memb_nodes), (stiff_hbm, stiff), (cols_hbm, cols)))
    ]
    for copy in small:
        copy.start()

    barrier = pltpu.get_barrier_semaphore()
    for i in range(gys):
        @pl.when(i != y)
        def _():
            pl.semaphore_signal(barrier, inc=1, device_id=(g, x, i), device_id_type=MESH)
    for p in range(groups * gxs):
        @pl.when(p != plane)
        def _():
            pl.semaphore_signal(barrier, inc=1, device_id=(p // gxs, p % gxs, y), device_id_type=MESH)

    def peer(c):
        return (jnp.where(rod, c // gys + 1, 0), x, c % gys)

    def each_chunk(body):
        for c in range(chunks):
            if c < gys:
                body(c)
            else:
                pl.when(rod)(functools.partial(body, c))

    each_chunk(lambda c: pl.semaphore_signal(barrier, inc=1, device_id=peer(c), device_id_type=MESH))

    sides = (
        (nb - 1, x < gxs - 1, lambda: (g, x + 1, y), x > 0, lambda: (g, x - 1, y)),
        (0, x > 0, lambda: (g, x - 1, y), x < gxs - 1, lambda: (g, x + 1, y)),
        (1, y < gys - 1, lambda: (g, x, y + 1), y > 0, lambda: (g, x, y - 1)),
        (nb - 2, y > 0, lambda: (g, x, y - 1), y < gys - 1, lambda: (g, x, y + 1)),
    )
    for r in order[:4]:
        pltpu.make_async_copy(v_hbm.at[r], acc0.at[r], v_sem.at[r]).wait()
        ext[0, r] = acc0[r].astype(BF16)

    pl.semaphore_wait(barrier, gys - 1 + groups * gxs - 1 + jnp.where(rod, chunks, gys))

    def side_copy(s, d, device):
        return pltpu.make_async_remote_copy(
            src_ref=ext.at[lax.rem(s, 2), sides[d][0]], dst_ref=land.at[s, d],
            send_sem=gs.at[s, d], recv_sem=gr.at[s, d],
            device_id=device, device_id_type=MESH)

    def send_sides(s, more=True):
        for d, (_, sends, to, _, _) in enumerate(sides):
            @pl.when(sends & more)
            def _():
                side_copy(s, d, to()).start()

    def wait_sides(s):
        for d, (_, _, _, hears, source) in enumerate(sides):
            @pl.when(hears)
            def _():
                side_copy(s, d, source()).wait_recv()
        for d, (_, sends, to, _, _) in enumerate(sides):
            ext[lax.rem(s, 2), nb + d] = land[s, d]

            @pl.when(sends)
            def _():
                side_copy(s, d, to()).wait_send()

    my_chunk = jnp.where(rod, y, (g - 1) * gys + y)

    def sleeve_copy(s, c, dst):
        return pltpu.make_async_remote_copy(
            src_ref=own.at[s, c // gys, c % gys], dst_ref=oth.at[s, dst // gys, dst % gys],
            send_sem=ss.at[s, c], recv_sem=sr.at[s, dst],
            device_id=peer(c), device_id_type=MESH)

    def kap_copy(c, dst):
        return pltpu.make_async_remote_copy(
            src_ref=kown.at[c % gys], dst_ref=kap.at[dst // gys, dst % gys],
            send_sem=ks.at[c % gys], recv_sem=kr.at[dst],
            device_id=peer(c), device_id_type=MESH)

    send_sides(0)
    for copy in small:
        copy.wait()

    for d, (_, _, _, hears, _) in enumerate(sides):
        @pl.when(jnp.logical_not(hears))
        def _():
            for s in range(MATVECS):
                land[s, d] = jnp.zeros((width, lanes), BF16)

    cap = rows // DOFS
    member = jnp.maximum(g - 1, 0)
    slot = lax.broadcasted_iota(jnp.int32, (cap, lanes), 0)
    for c in range(gys):
        value = jnp.zeros((cap, lanes), F32)
        for t in range(cap):
            value = jnp.where(slot == t, stiff[c, member, 0, t], value)
        for d in range(DOFS):
            kown[c, d * cap:(d + 1) * cap] = value

    @pl.when(jnp.logical_not(rod))
    def _():
        kap[0] = kown[...]
        for m in range(1, members):
            kap[m] = jnp.zeros((gys, rows, lanes), F32)
            for s in range(MATVECS):
                oth[s, m] = jnp.zeros((gys, rows, lanes), BF16)

    def node_of(m, c, t):
        return jnp.where(rod, rod_nodes[m, c, t], jnp.where(m == 0, memb_nodes[c, member, 0, t], -1))

    def gather_matrix(m, carry):
        for c in range(gys):
            value = jnp.zeros((cap, lanes), jnp.int32)
            for t in range(cap):
                value = jnp.where(slot == t, node_of(m, c, t), value)
            wanted = jnp.concatenate(
                [jnp.where(value >= 0, value * DOFS + d, -1) for d in range(DOFS)], axis=0)
            lane = lax.broadcasted_iota(jnp.int32, (rows, lanes), 1)
            for b in range(nb * width // lanes):
                hot = jnp.where(wanted == lane + b * lanes, F32(1.0), F32(0.0)).astype(BF16)
                gat[m, c * rows:(c + 1) * rows, b * lanes:(b + 1) * lanes] = hot
        return carry

    lax.fori_loop(0, members, gather_matrix, 0)


    @pl.when(jnp.logical_not(rod))
    def _():
        for c in range(gys):
            kap_copy(c, my_chunk).start()

    for r in order[4:]:
        pltpu.make_async_copy(v_hbm.at[r], acc0.at[r], v_sem.at[r]).wait()
        ext[0, r] = acc0[r].astype(BF16)

    def gather(s):
        def one(m, carry):
            got = jnp.dot(gat[m], ext[lax.rem(s, 2), :nb].reshape(nb * width, lanes), preferred_element_type=F32)
            own[s, m] = got.astype(BF16).reshape(gys, rows, lanes)
            return carry

        lax.fori_loop(0, members, one, 0)
        each_chunk(lambda c: sleeve_copy(s, c, my_chunk).start())

    early = width // 256 * 256

    def first_blocks(s):
        def one(r, carry):
            acc0[r] = jnp.dot(a[r, 0, :, :early], ext[lax.rem(s, 2), r, :early], preferred_element_type=F32)
            return carry

        lax.fori_loop(0, nb, one, 0, unroll=4)

    def spring_forces(s):
        each_chunk(lambda c: sleeve_copy(s, c, c).wait_recv())
        for m in range(members):
            force = kap[m] * (own[s, m].astype(F32) - oth[s, m].astype(F32))
            dlt[m * gys * rows:(m + 1) * gys * rows] = force.astype(BF16).reshape(gys * rows, lanes)

    def main_rows(s, half):
        now = lax.rem(s, 2)

        def one(i, carry):
            r = row_of(half * 4 + i)
            left = jnp.concatenate(
                [a[r, 0, :, early:]] + [a[r, k] for k in range(1, kb)] + [sca[r]], axis=1)
            right = jnp.concatenate(
                [ext[now, r, early:]] + [ext[now, cols[k, r]] for k in range(1, kb)] + [dlt[...]], axis=0)
            c = (acc0[r] + jnp.dot(left, right, preferred_element_type=F32)) * inv[...]
            sqacc[...] += jnp.sum((c * c).reshape(width // 8, 8, lanes), axis=0)
            ext[1 - now, r] = c.astype(BF16)
            acc0[r] = c
            return carry

        lax.fori_loop(0, 4, one, 0, unroll=2)

    def line_copy(s, i, slot):
        return pltpu.make_async_remote_copy(
            src_ref=sqa.at[s, y], dst_ref=sqa.at[s, slot],
            send_sem=as_.at[s, i], recv_sem=ar.at[s, slot],
            device_id=(g, x, i), device_id_type=MESH)

    def plane_copy(s, p, slot):
        return pltpu.make_async_remote_copy(
            src_ref=sqb.at[s, plane], dst_ref=sqb.at[s, slot],
            send_sem=bs.at[s, p], recv_sem=br.at[s, slot],
            device_id=(p // gxs, p % gxs, y), device_id_type=MESH)

    def squares_line(s):
        sqa[s, y] = sqacc[...]
        for i in range(gys):
            @pl.when(i != y)
            def _():
                line_copy(s, i, y).start()

    def squares_plane(s):
        for i in range(gys):
            @pl.when(i != y)
            def _():
                line_copy(s, i, i).wait_recv()
        total = sqa[s, 0]
        for i in range(1, gys):
            total = total + sqa[s, i]
        sqb[s, plane] = total
        for p in range(groups * gxs):
            @pl.when(p != plane)
            def _():
                plane_copy(s, p, plane).start()

    def squares_end(s):
        for p in range(groups * gxs):
            @pl.when(p != plane)
            def _():
                plane_copy(s, p, p).wait_recv()
        total = sqb[s, 0]
        for p in range(1, groups * gxs):
            total = total + sqb[s, p]
        scale = jnp.sqrt(jnp.sum(total, axis=0, keepdims=True) / all_dofs + EPSILON)
        norms[pl.ds(s, 1), :] = scale
        inv[...] = 1.0 / scale

    padded = sca.shape[2]
    place = lax.broadcasted_iota(jnp.int32, (8, padded), 1)
    within = lax.rem(place, rows)
    key = lax.div(place, rows) * cap + lax.rem(within, cap)

    def slot_row(j, value):
        c = lax.div(j, cap)
        node = node_of(lax.div(c, gys), lax.rem(c, gys), lax.rem(j, cap))
        return jnp.where(key == j, node, value)

    node_row = lax.fori_loop(0, chunks * cap, slot_row, jnp.full((8, padded), -1, jnp.int32))
    node_row = jnp.where(node_row >= 0, node_row * DOFS + lax.div(within, cap), -1)

    def scatter_matrix(r, carry):
        dof = lax.broadcasted_iota(jnp.int32, (width, padded), 0) + r * width
        sca[r] = jnp.where(node_row[:1] == dof, F32(1.0), F32(0.0)).astype(BF16)
        return carry

    lax.fori_loop(0, nb, scatter_matrix, 0)
    if dlt.shape[0] > chunks * rows:
        dlt[chunks * rows:] = jnp.zeros((dlt.shape[0] - chunks * rows, lanes), BF16)
    inv[...] = jnp.ones_like(inv)
    last = MATVECS - 1

    def step(s, carry):
        gather(s)

        @pl.when(s == 0)
        def _():
            pltpu.make_async_copy(a_hbm.at[:, 0], a.at[:, 0], a0_sem).wait()

        first_blocks(s)

        @pl.when(s > 0)
        def _():
            squares_plane(s - 1)

        @pl.when((s == 0) & rod)
        def _():
            for c in range(chunks):
                kap_copy(c, c).wait_recv()

        spring_forces(s)
        wait_sides(s)

        @pl.when(s > 0)
        def _():
            squares_end(s - 1)

        @pl.when(s == 0)
        def _():
            for r in order:
                pltpu.make_async_copy(
                    a_hbm.at[r, pl.ds(1, kb - 1)], a.at[r, pl.ds(1, kb - 1)], a_sem.at[r]).wait()

        sqacc[...] = jnp.zeros_like(sqacc)

        def part(half, carry):
            main_rows(s, half)
            send_sides(s + 1, (half == 0) & (s < last))
            return carry

        lax.fori_loop(0, nb // 4, part, 0)
        squares_line(s)
        return carry

    lax.fori_loop(0, MATVECS, step, 0)
    squares_plane(last)

    def sent(s, carry):
        each_chunk(lambda c: sleeve_copy(s, c, c).wait_send())
        for i in range(gys):
            @pl.when(i != y)
            def _():
                line_copy(s, i, y).wait_send()
        for p in range(groups * gxs):
            @pl.when(p != plane)
            def _():
                plane_copy(s, p, plane).wait_send()
        return carry

    lax.fori_loop(0, MATVECS, sent, 0)

    @pl.when(jnp.logical_not(rod))
    def _():
        for c in range(gys):
            kap_copy(c, c).wait_send()

    squares_end(last)
    for r in range(nb):
        result[r] = acc0[r] * inv[...]


def local(groups, gxs, gys, start_vectors, tile_blocks, block_columns, sleeve_rod, sleeve_membrane, sleeve_stiffness):
    nb, kb, width = tile_blocks.shape[3:6]
    lanes = start_vectors.shape[5]
    cap = sleeve_rod.shape[4]
    members = groups - 1
    rows = cap * DOFS
    chunks = members * gys
    slot_rows = chunks * rows
    padded = -(-slot_rows // 256) * 256
    small = (block_columns[0, 0, 0].T, sleeve_rod[0, 0], sleeve_membrane[0], sleeve_stiffness[0])
    vmem = pl.BlockSpec(memory_space=pltpu.VMEM)
    hbm = pl.BlockSpec(memory_space=pl.ANY)
    dma = pltpu.SemaphoreType.DMA
    plane = groups * gxs
    flops = 2 * MATVECS * nb * kb * width * width * lanes
    final, norms = pl.pallas_call(
        functools.partial(kernel, groups, gxs, gys, nb, kb, width, lanes, rows),
        out_shape=(
            pltpu.VMEM((nb, width, lanes), F32),
            pltpu.VMEM((MATVECS, lanes), F32),
        ),
        in_specs=[hbm] * 6,
        out_specs=(vmem, vmem),
        scratch_shapes=[
            *[pltpu.SMEM(array.shape, array.dtype) for array in small],
            pltpu.VMEM((nb, kb, width, width), BF16),
            pltpu.VMEM((2, nb + 4, width, lanes), BF16),
            pltpu.VMEM((MATVECS, 4, width, lanes), BF16),
            pltpu.VMEM((nb, width, lanes), F32),
            pltpu.VMEM((members, gys * rows, nb * width), BF16),
            pltpu.VMEM((nb, width, padded), BF16),
            pltpu.VMEM((MATVECS, members, gys, rows, lanes), BF16),
            pltpu.VMEM((MATVECS, members, gys, rows, lanes), BF16),
            pltpu.VMEM((gys, rows, lanes), F32),
            pltpu.VMEM((members, gys, rows, lanes), F32),
            pltpu.VMEM((padded, lanes), BF16),
            pltpu.VMEM((8, lanes), F32),
            pltpu.VMEM((MATVECS, gys, 8, lanes), F32),
            pltpu.VMEM((MATVECS, plane, 8, lanes), F32),
            pltpu.VMEM((1, lanes), F32),
            dma((4,)), dma((nb,)), dma, dma((nb,)),
            dma((MATVECS, 4)), dma((MATVECS, 4)),
            dma((MATVECS, chunks)), dma((MATVECS, chunks)),
            dma((gys,)), dma((chunks,)),
            dma((MATVECS, gys)), dma((MATVECS, gys)),
            dma((MATVECS, plane)), dma((MATVECS, plane)),
        ],
        compiler_params=pltpu.CompilerParams(
            collective_id=0, has_side_effects=True, vmem_limit_bytes=58 * 2**20),
        cost_estimate=pl.CostEstimate(flops=flops, bytes_accessed=tile_blocks.size * 2, transcendentals=0),
    )(*small,
      start_vectors.reshape(nb, width, lanes), tile_blocks.reshape(nb, kb, width, width))
    return (final[None, None, None], norms)


def solution(mesh):
    return jax.shard_map(
        functools.partial(local, mesh.shape["group"], mesh.shape["gx"], mesh.shape["gy"]),
        mesh=mesh,
        in_specs=(
            P("group", "gx", "gy", None, None, None),
            P("group", "gx", "gy", None, None, None, None),
            P("group", "gx", "gy", None, None),
            P("gx", "gy", None, None, None),
            P("gx", None, None, "gy", None),
            P("gx", None, None, "gy", None),
        ),
        out_specs=(P("group", "gx", "gy", None, None, None), P()),
        check_vma=False,
    )
```

```python
import functools

import jax
import jax.numpy as jnp
from jax import lax
from jax.experimental import pallas as pl
from jax.experimental.pallas import tpu as pltpu
from jax.sharding import PartitionSpec as P

MATVECS = 3
DOFS = 6
EPSILON = 1e-06
MESH = pl.DeviceIdType.MESH
F32 = jnp.float32
BF16 = jnp.bfloat16


def kernel(groups, gxs, gys, nb, kb, width, lanes, rows,
           cols_hbm, rod_hbm, memb_hbm, stiff_hbm, v_hbm, a_hbm,
           result, norms,
           cols, rod_nodes, memb_nodes, stiff, a, ext, land, rel, acc0, gat, sca, own, oth, kown, kap, dlt, sqacc, sqa, sqb, inv,
           i_sem, v_sem, a0_sem, a_sem, gs, gr, rs, rr, fs, fr, ss, sr, ks, kr, as_, ar, bs, br):
    g = lax.axis_index("group")
    x = lax.axis_index("gx")
    y = lax.axis_index("gy")
    plane = g * gxs + x
    rod = g == 0
    members = groups - 1
    chunks = members * gys
    all_dofs = float(groups * gxs * gys * nb * width)

    def row_of(i):
        half, odd = lax.div(i, 2), lax.rem(i, 2)
        return half * (1 - 2 * odd) + odd * (nb - 1)

    order = [i // 2 if i % 2 == 0 else nb - 1 - i // 2 for i in range(nb)]
    for r in order:
        pltpu.make_async_copy(v_hbm.at[r], acc0.at[r], v_sem.at[r]).start()
    pltpu.make_async_copy(a_hbm.at[:, 0], a.at[:, 0], a0_sem).start()
    for r in order:
        pltpu.make_async_copy(a_hbm.at[r, pl.ds(1, kb - 1)], a.at[r, pl.ds(1, kb - 1)], a_sem.at[r]).start()

    small = [
        pltpu.make_async_copy(src, dst, i_sem.at[i])
        for i, (src, dst) in enumerate(
            ((rod_hbm, rod_nodes), (memb_hbm, memb_nodes), (stiff_hbm, stiff), (cols_hbm, cols)))
    ]
    for copy in small:
        copy.start()

    barrier = pltpu.get_barrier_semaphore()
    for i in range(gys):
        @pl.when(i != y)
        def _():
            pl.semaphore_signal(barrier, inc=1, device_id=(g, x, i), device_id_type=MESH)
    for p in range(groups * gxs):
        @pl.when(p != plane)
        def _():
            pl.semaphore_signal(barrier, inc=1, device_id=(p // gxs, p % gxs, y), device_id_type=MESH)

    def peer(c):
        return (jnp.where(rod, c // gys + 1, 0), x, c % gys)

    def each_chunk(body):
        for c in range(chunks):
            if c < gys:
                body(c)
            else:
                pl.when(rod)(functools.partial(body, c))

    each_chunk(lambda c: pl.semaphore_signal(barrier, inc=1, device_id=peer(c), device_id_type=MESH))

    sides = (
        (nb - 1, x < gxs - 1, lambda: (g, x + 1, y), x > 0, lambda: (g, x - 1, y)),
        (0, x > 0, lambda: (g, x - 1, y), x < gxs - 1, lambda: (g, x + 1, y)),
        (1, y < gys - 1, lambda: (g, x, y + 1), y > 0, lambda: (g, x, y - 1)),
        (nb - 2, y > 0, lambda: (g, x, y - 1), y < gys - 1, lambda: (g, x, y + 1)),
    )
    for r in order[:4]:
        pltpu.make_async_copy(v_hbm.at[r], acc0.at[r], v_sem.at[r]).wait()
        ext[0, r] = acc0[r].astype(BF16)

    pl.semaphore_wait(barrier, gys - 1 + groups * gxs - 1 + jnp.where(rod, chunks, gys))

    relay = groups == 2 and gxs == 4
    cut = width // 2
    far = ((x == 1), (x == 2), None, None)
    far_hears = ((x == 2), (x == 1), None, None)

    def side_copy(s, d, device, part=slice(None)):
        return pltpu.make_async_remote_copy(
            src_ref=ext.at[lax.rem(s, 2), sides[d][0], part], dst_ref=land.at[s, d, part],
            send_sem=gs.at[s, d], recv_sem=gr.at[s, d],
            device_id=device, device_id_type=MESH)

    def relay_copy(s):
        return pltpu.make_async_remote_copy(
            src_ref=ext.at[lax.rem(s, 2), jnp.where(x == 1, nb - 1, 0), pl.ds(cut, cut)], dst_ref=rel.at[s],
            send_sem=rs.at[s], recv_sem=rr.at[s],
            device_id=(g, jnp.where(x == 1, 3, jnp.where(x == 2, 0, jnp.where(x == 0, 2, 1))), y),
            device_id_type=MESH)

    def forward_copy(s):
        side = jnp.where((x == 3) | (x == 2), 0, 1)
        return pltpu.make_async_remote_copy(
            src_ref=rel.at[s], dst_ref=land.at[s, side, pl.ds(cut, cut)],
            send_sem=fs.at[s], recv_sem=fr.at[s],
            device_id=(g, jnp.where(x == 3, 2, jnp.where(x == 2, 3, jnp.where(x == 0, 1, 0))), y),
            device_id_type=MESH)

    middle = (x == 1) | (x == 2)

    def side_case(d, condition, is_far, whole, halved):
        if relay and d < 2:
            pl.when(condition & jnp.logical_not(is_far))(whole)
            pl.when(condition & is_far)(halved)
        else:
            pl.when(condition)(whole)

    def send_sides(s, which, more=True):
        for d in which:
            _, sends, to, _, _ = sides[d]

            def whole():
                side_copy(s, d, to()).start()

            def halved():
                relay_copy(s).start()
                side_copy(s, d, to(), pl.ds(0, cut)).start()

            side_case(d, sends & more, far[d], whole, halved)

    def forward(s):
        if relay:
            @pl.when(jnp.logical_not(middle))
            def _():
                relay_copy(s).wait_recv()
                forward_copy(s).start()

    def wait_sides(s):
        for d, (_, sends, to, hears, source) in enumerate(sides):
            def whole():
                side_copy(s, d, source()).wait_recv()

            def halved():
                side_copy(s, d, source(), pl.ds(0, cut)).wait_recv()
                forward_copy(s).wait_recv()

            side_case(d, hears, far_hears[d], whole, halved)
        for d, (_, sends, to, _, _) in enumerate(sides):
            ext[lax.rem(s, 2), nb + d] = land[s, d]

            def whole_sent():
                side_copy(s, d, to()).wait_send()

            def halved_sent():
                relay_copy(s).wait_send()
                side_copy(s, d, to(), pl.ds(0, cut)).wait_send()

            side_case(d, sends, far[d], whole_sent, halved_sent)
        if relay:
            @pl.when(jnp.logical_not(middle))
            def _():
                forward_copy(s).wait_send()

    my_chunk = jnp.where(rod, y, (g - 1) * gys + y)

    def sleeve_copy(s, c, dst):
        return pltpu.make_async_remote_copy(
            src_ref=own.at[s, c // gys, c % gys], dst_ref=oth.at[s, dst // gys, dst % gys],
            send_sem=ss.at[s, c], recv_sem=sr.at[s, dst],
            device_id=peer(c), device_id_type=MESH)

    def kap_copy(c, dst):
        return pltpu.make_async_remote_copy(
            src_ref=kown.at[c % gys], dst_ref=kap.at[dst // gys, dst % gys],
            send_sem=ks.at[c % gys], recv_sem=kr.at[dst],
            device_id=peer(c), device_id_type=MESH)

    send_sides(0, (0, 1, 2, 3))
    for copy in small:
        copy.wait()

    for d, (_, _, _, hears, _) in enumerate(sides):
        @pl.when(jnp.logical_not(hears))
        def _():
            for s in range(MATVECS):
                land[s, d] = jnp.zeros((width, lanes), BF16)

    cap = rows // DOFS
    member = jnp.maximum(g - 1, 0)
    slot = lax.broadcasted_iota(jnp.int32, (cap, lanes), 0)
    for c in range(gys):
        value = jnp.zeros((cap, lanes), F32)
        for t in range(cap):
            value = jnp.where(slot == t, stiff[c, member, 0, t], value)
        for d in range(DOFS):
            kown[c, d * cap:(d + 1) * cap] = value

    @pl.when(jnp.logical_not(rod))
    def _():
        kap[0] = kown[...]
        for m in range(1, members):
            kap[m] = jnp.zeros((gys, rows, lanes), F32)
            for s in range(MATVECS):
                oth[s, m] = jnp.zeros((gys, rows, lanes), BF16)

    def node_of(m, c, t):
        return jnp.where(rod, rod_nodes[m, c, t], jnp.where(m == 0, memb_nodes[c, member, 0, t], -1))

    def gather_matrix(m, carry):
        for c in range(gys):
            value = jnp.zeros((cap, lanes), jnp.int32)
            for t in range(cap):
                value = jnp.where(slot == t, node_of(m, c, t), value)
            wanted = jnp.concatenate(
                [jnp.where(value >= 0, value * DOFS + d, -1) for d in range(DOFS)], axis=0)
            lane = lax.broadcasted_iota(jnp.int32, (rows, lanes), 1)
            for b in range(nb * width // lanes):
                hot = jnp.where(wanted == lane + b * lanes, F32(1.0), F32(0.0)).astype(BF16)
                gat[m, c * rows:(c + 1) * rows, b * lanes:(b + 1) * lanes] = hot
        return carry

    lax.fori_loop(0, members, gather_matrix, 0)


    @pl.when(jnp.logical_not(rod))
    def _():
        for c in range(gys):
            kap_copy(c, my_chunk).start()

    for r in order[4:]:
        pltpu.make_async_copy(v_hbm.at[r], acc0.at[r], v_sem.at[r]).wait()
        ext[0, r] = acc0[r].astype(BF16)

    def gather(s):
        def one(m, carry):
            got = jnp.dot(gat[m], ext[lax.rem(s, 2), :nb].reshape(nb * width, lanes), preferred_element_type=F32)
            own[s, m] = got.astype(BF16).reshape(gys, rows, lanes)
            return carry

        lax.fori_loop(0, members, one, 0)
        each_chunk(lambda c: sleeve_copy(s, c, my_chunk).start())

    early = width // 256 * 256

    def first_blocks(s):
        def one(r, carry):
            acc0[r] = jnp.dot(a[r, 0, :, :early], ext[lax.rem(s, 2), r, :early], preferred_element_type=F32)
            return carry

        lax.fori_loop(0, nb, one, 0, unroll=4)

    def spring_forces(s):
        each_chunk(lambda c: sleeve_copy(s, c, c).wait_recv())
        for m in range(members):
            force = kap[m] * (own[s, m].astype(F32) - oth[s, m].astype(F32))
            dlt[m * gys * rows:(m + 1) * gys * rows] = force.astype(BF16).reshape(gys * rows, lanes)

    def main_rows(s, pair):
        now = lax.rem(s, 2)

        def one(i, carry):
            r = row_of(pair * 2 + i)
            left = jnp.concatenate(
                [a[r, 0, :, early:]] + [a[r, k] for k in range(1, kb)] + [sca[r]], axis=1)
            right = jnp.concatenate(
                [ext[now, r, early:]] + [ext[now, cols[k, r]] for k in range(1, kb)] + [dlt[...]], axis=0)
            c = (acc0[r] + jnp.dot(left, right, preferred_element_type=F32)) * inv[...]
            sqacc[...] += jnp.sum((c * c).reshape(width // 8, 8, lanes), axis=0)
            ext[1 - now, r] = c.astype(BF16)
            acc0[r] = c
            return carry

        lax.fori_loop(0, 2, one, 0, unroll=2)

    def line_copy(s, i, slot):
        return pltpu.make_async_remote_copy(
            src_ref=sqa.at[s, y], dst_ref=sqa.at[s, slot],
            send_sem=as_.at[s, i], recv_sem=ar.at[s, slot],
            device_id=(g, x, i), device_id_type=MESH)

    def plane_copy(s, p, slot):
        return pltpu.make_async_remote_copy(
            src_ref=sqb.at[s, plane], dst_ref=sqb.at[s, slot],
            send_sem=bs.at[s, p], recv_sem=br.at[s, slot],
            device_id=(p // gxs, p % gxs, y), device_id_type=MESH)

    def squares_line(s):
        sqa[s, y] = sqacc[...]
        for i in range(gys):
            @pl.when(i != y)
            def _():
                line_copy(s, i, y).start()

    def squares_plane(s):
        for i in range(gys):
            @pl.when(i != y)
            def _():
                line_copy(s, i, i).wait_recv()
        total = sqa[s, 0]
        for i in range(1, gys):
            total = total + sqa[s, i]
        sqb[s, plane] = total
        for p in range(groups * gxs):
            @pl.when(p != plane)
            def _():
                plane_copy(s, p, plane).start()

    def squares_end(s):
        for p in range(groups * gxs):
            @pl.when(p != plane)
            def _():
                plane_copy(s, p, p).wait_recv()
        total = sqb[s, 0]
        for p in range(1, groups * gxs):
            total = total + sqb[s, p]
        scale = jnp.sqrt(jnp.sum(total, axis=0, keepdims=True) / all_dofs + EPSILON)
        norms[pl.ds(s, 1), :] = scale
        inv[...] = 1.0 / scale

    padded = sca.shape[2]
    place = lax.broadcasted_iota(jnp.int32, (8, padded), 1)
    within = lax.rem(place, rows)
    key = lax.div(place, rows) * cap + lax.rem(within, cap)

    def slot_row(j, value):
        c = lax.div(j, cap)
        node = node_of(lax.div(c, gys), lax.rem(c, gys), lax.rem(j, cap))
        return jnp.where(key == j, node, value)

    node_row = lax.fori_loop(0, chunks * cap, slot_row, jnp.full((8, padded), -1, jnp.int32))
    node_row = jnp.where(node_row >= 0, node_row * DOFS + lax.div(within, cap), -1)

    def scatter_matrix(r, carry):
        dof = lax.broadcasted_iota(jnp.int32, (width, padded), 0) + r * width
        sca[r] = jnp.where(node_row[:1] == dof, F32(1.0), F32(0.0)).astype(BF16)
        return carry

    lax.fori_loop(0, nb, scatter_matrix, 0)
    if dlt.shape[0] > chunks * rows:
        dlt[chunks * rows:] = jnp.zeros((dlt.shape[0] - chunks * rows, lanes), BF16)
    inv[...] = jnp.ones_like(inv)
    last = MATVECS - 1

    def step(s, carry):
        gather(s)
        forward(s)

        @pl.when(s == 0)
        def _():
            pltpu.make_async_copy(a_hbm.at[:, 0], a.at[:, 0], a0_sem).wait()

        first_blocks(s)

        @pl.when(s > 0)
        def _():
            squares_plane(s - 1)

        @pl.when((s == 0) & rod)
        def _():
            for c in range(chunks):
                kap_copy(c, c).wait_recv()

        spring_forces(s)
        wait_sides(s)

        @pl.when(s > 0)
        def _():
            squares_end(s - 1)

        @pl.when(s == 0)
        def _():
            for r in order:
                pltpu.make_async_copy(
                    a_hbm.at[r, pl.ds(1, kb - 1)], a.at[r, pl.ds(1, kb - 1)], a_sem.at[r]).wait()

        sqacc[...] = jnp.zeros_like(sqacc)

        def part(pair, carry):
            main_rows(s, pair)
            send_sides(s + 1, (0, 1), (pair == 0) & (s < last))
            send_sides(s + 1, (2, 3), (pair == 1) & (s < last))
            return carry

        lax.fori_loop(0, nb // 2, part, 0)
        squares_line(s)
        return carry

    lax.fori_loop(0, MATVECS, step, 0)
    squares_plane(last)

    def sent(s, carry):
        each_chunk(lambda c: sleeve_copy(s, c, c).wait_send())
        for i in range(gys):
            @pl.when(i != y)
            def _():
                line_copy(s, i, y).wait_send()
        for p in range(groups * gxs):
            @pl.when(p != plane)
            def _():
                plane_copy(s, p, plane).wait_send()
        return carry

    lax.fori_loop(0, MATVECS, sent, 0)

    @pl.when(jnp.logical_not(rod))
    def _():
        for c in range(gys):
            kap_copy(c, c).wait_send()

    squares_end(last)
    for r in range(nb):
        result[r] = acc0[r] * inv[...]


def local(groups, gxs, gys, start_vectors, tile_blocks, block_columns, sleeve_rod, sleeve_membrane, sleeve_stiffness):
    nb, kb, width = tile_blocks.shape[3:6]
    lanes = start_vectors.shape[5]
    cap = sleeve_rod.shape[4]
    members = groups - 1
    rows = cap * DOFS
    chunks = members * gys
    slot_rows = chunks * rows
    padded = -(-slot_rows // 256) * 256
    small = (block_columns[0, 0, 0].T, sleeve_rod[0, 0], sleeve_membrane[0], sleeve_stiffness[0])
    vmem = pl.BlockSpec(memory_space=pltpu.VMEM)
    hbm = pl.BlockSpec(memory_space=pl.ANY)
    dma = pltpu.SemaphoreType.DMA
    plane = groups * gxs
    flops = 2 * MATVECS * nb * kb * width * width * lanes
    final, norms = pl.pallas_call(
        functools.partial(kernel, groups, gxs, gys, nb, kb, width, lanes, rows),
        out_shape=(
            pltpu.VMEM((nb, width, lanes), F32),
            pltpu.VMEM((MATVECS, lanes), F32),
        ),
        in_specs=[hbm] * 6,
        out_specs=(vmem, vmem),
        scratch_shapes=[
            *[pltpu.SMEM(array.shape, array.dtype) for array in small],
            pltpu.VMEM((nb, kb, width, width), BF16),
            pltpu.VMEM((2, nb + 4, width, lanes), BF16),
            pltpu.VMEM((MATVECS, 4, width, lanes), BF16),
            pltpu.VMEM((MATVECS, width // 2, lanes), BF16),
            pltpu.VMEM((nb, width, lanes), F32),
            pltpu.VMEM((members, gys * rows, nb * width), BF16),
            pltpu.VMEM((nb, width, padded), BF16),
            pltpu.VMEM((MATVECS, members, gys, rows, lanes), BF16),
            pltpu.VMEM((MATVECS, members, gys, rows, lanes), BF16),
            pltpu.VMEM((gys, rows, lanes), F32),
            pltpu.VMEM((members, gys, rows, lanes), F32),
            pltpu.VMEM((padded, lanes), BF16),
            pltpu.VMEM((8, lanes), F32),
            pltpu.VMEM((MATVECS, gys, 8, lanes), F32),
            pltpu.VMEM((MATVECS, plane, 8, lanes), F32),
            pltpu.VMEM((1, lanes), F32),
            dma((4,)), dma((nb,)), dma, dma((nb,)),
            dma((MATVECS, 4)), dma((MATVECS, 4)),
            *[dma((MATVECS,))] * 4,
            dma((MATVECS, chunks)), dma((MATVECS, chunks)),
            dma((gys,)), dma((chunks,)),
            dma((MATVECS, gys)), dma((MATVECS, gys)),
            dma((MATVECS, plane)), dma((MATVECS, plane)),
        ],
        compiler_params=pltpu.CompilerParams(
            collective_id=0, has_side_effects=True, vmem_limit_bytes=58 * 2**20),
        cost_estimate=pl.CostEstimate(flops=flops, bytes_accessed=tile_blocks.size * 2, transcendentals=0),
    )(*small,
      start_vectors.reshape(nb, width, lanes), tile_blocks.reshape(nb, kb, width, width))
    return (final[None, None, None], norms)


def solution(mesh):
    return jax.shard_map(
        functools.partial(local, mesh.shape["group"], mesh.shape["gx"], mesh.shape["gy"]),
        mesh=mesh,
        in_specs=(
            P("group", "gx", "gy", None, None, None),
            P("group", "gx", "gy", None, None, None, None),
            P("group", "gx", "gy", None, None),
            P("gx", "gy", None, None, None),
            P("gx", None, None, "gy", None),
            P("gx", None, None, "gy", None),
        ),
        out_specs=(P("group", "gx", "gy", None, None, None), P()),
        check_vma=False,
    )
```

```python
import functools

import jax
import jax.numpy as jnp
from jax import lax
from jax.experimental import pallas as pl
from jax.experimental.pallas import tpu as pltpu
from jax.sharding import PartitionSpec as P

MATVECS = 3
DOFS = 6
EPSILON = 1e-06
MESH = pl.DeviceIdType.MESH
F32 = jnp.float32
BF16 = jnp.bfloat16


def kernel(groups, gxs, gys, nb, kb, width, lanes, rows,
           cols_hbm, rod_hbm, memb_hbm, stiff_hbm, v_hbm, a_hbm,
           result, norms,
           cols, rod_nodes, memb_nodes, stiff, a, ext, land, acc0, gat, sca, own, oth, kown, kap, dlt, sqacc, sqa, sqb, inv,
           i_sem, v_sem, a0_sem, a_sem, gs, gr, ss, sr, ks, kr, as_, ar, bs, br):
    g = lax.axis_index("group")
    x = lax.axis_index("gx")
    y = lax.axis_index("gy")
    plane = g * gxs + x
    rod = g == 0
    members = groups - 1
    chunks = members * gys
    all_dofs = float(groups * gxs * gys * nb * width)

    def row_of(i):
        half, odd = lax.div(i, 2), lax.rem(i, 2)
        return half * (1 - 2 * odd) + odd * (nb - 1)

    order = [i // 2 if i % 2 == 0 else nb - 1 - i // 2 for i in range(nb)]
    for r in order:
        pltpu.make_async_copy(v_hbm.at[r], acc0.at[r], v_sem.at[r]).start()
    pltpu.make_async_copy(a_hbm.at[:, 0], a.at[:, 0], a0_sem).start()
    rest = pltpu.make_async_copy(a_hbm.at[:, pl.ds(1, kb - 1)], a.at[:, pl.ds(1, kb - 1)], a_sem)
    rest.start()

    small = [
        pltpu.make_async_copy(src, dst, i_sem.at[i])
        for i, (src, dst) in enumerate(
            ((rod_hbm, rod_nodes), (memb_hbm, memb_nodes), (stiff_hbm, stiff), (cols_hbm, cols)))
    ]
    for copy in small:
        copy.start()

    barrier = pltpu.get_barrier_semaphore()
    n_plane = groups * gxs

    def line_peer(i):
        return (g, x, lax.rem(y + i, gys))

    def plane_peer(i):
        p = lax.rem(plane + i, n_plane)
        return (lax.div(p, gxs), lax.rem(p, gxs), y)

    for i in range(1, gys):
        pl.semaphore_signal(barrier, inc=1, device_id=line_peer(i), device_id_type=MESH)
    for i in range(1, n_plane):
        pl.semaphore_signal(barrier, inc=1, device_id=plane_peer(i), device_id_type=MESH)

    def peer(c):
        return (1 - g if members == 1 else jnp.where(rod, c // gys + 1, 0), x, c % gys)

    def each_chunk(body):
        for c in range(chunks):
            if c < gys:
                body(c)
            else:
                pl.when(rod)(functools.partial(body, c))

    each_chunk(lambda c: pl.semaphore_signal(barrier, inc=1, device_id=peer(c), device_id_type=MESH))

    sides = (
        (nb - 1, x < gxs - 1, lambda: (g, x + 1, y), x > 0, lambda: (g, x - 1, y)),
        (0, x > 0, lambda: (g, x - 1, y), x < gxs - 1, lambda: (g, x + 1, y)),
        (1, y < gys - 1, lambda: (g, x, y + 1), y > 0, lambda: (g, x, y - 1)),
        (nb - 2, y > 0, lambda: (g, x, y - 1), y < gys - 1, lambda: (g, x, y + 1)),
    )
    for r in order[:4]:
        pltpu.make_async_copy(v_hbm.at[r], acc0.at[r], v_sem.at[r]).wait()
        ext[0, r] = acc0[r].astype(BF16)

    pl.semaphore_wait(barrier, gys - 1 + groups * gxs - 1 + jnp.where(rod, chunks, gys))

    def side_copy(s, d, device):
        return pltpu.make_async_remote_copy(
            src_ref=ext.at[lax.rem(s, 2), sides[d][0]], dst_ref=land.at[s, d],
            send_sem=gs.at[s, d], recv_sem=gr.at[s, d],
            device_id=device, device_id_type=MESH)

    def send_sides(s, more=True):
        for d, (_, sends, to, _, _) in enumerate(sides):
            @pl.when(sends & more)
            def _():
                side_copy(s, d, to()).start()

    def wait_sides(s):
        for d, (_, _, _, hears, source) in enumerate(sides):
            @pl.when(hears)
            def _():
                side_copy(s, d, source()).wait_recv()
        for d, (_, sends, to, _, _) in enumerate(sides):
            ext[lax.rem(s, 2), nb + d] = land[s, d]

            @pl.when(sends)
            def _():
                side_copy(s, d, to()).wait_send()

    my_chunk = jnp.where(rod, y, (g - 1) * gys + y)

    def sleeve_copy(s, c, dst):
        return pltpu.make_async_remote_copy(
            src_ref=own.at[s, c // gys, c % gys], dst_ref=oth.at[s, dst // gys, dst % gys],
            send_sem=ss.at[s], recv_sem=sr.at[s],
            device_id=peer(c), device_id_type=MESH)

    def kap_copy(c, dst):
        return pltpu.make_async_remote_copy(
            src_ref=kown.at[c % gys], dst_ref=kap.at[dst // gys, dst % gys],
            send_sem=ks, recv_sem=kr,
            device_id=peer(c), device_id_type=MESH)

    send_sides(0)
    for copy in small:
        copy.wait()

    for d, (_, _, _, hears, _) in enumerate(sides):
        @pl.when(jnp.logical_not(hears))
        def _():
            for s in range(MATVECS):
                land[s, d] = jnp.zeros((width, lanes), BF16)

    cap = rows // DOFS
    member = jnp.maximum(g - 1, 0)
    slot = lax.broadcasted_iota(jnp.int32, (cap, lanes), 0)
    for c in range(gys):
        value = jnp.zeros((cap, lanes), F32)
        for t in range(cap):
            value = jnp.where(slot == t, stiff[c, member, 0, t], value)
        for d in range(DOFS):
            kown[c, d * cap:(d + 1) * cap] = value

    @pl.when(jnp.logical_not(rod))
    def _():
        kap[0] = kown[...]
        for m in range(1, members):
            kap[m] = jnp.zeros((gys, rows, lanes), F32)
            for s in range(MATVECS):
                oth[s, m] = jnp.zeros((gys, rows, lanes), BF16)

    def node_of(m, c, t):
        return jnp.where(rod, rod_nodes[m, c, t], jnp.where(m == 0, memb_nodes[c, member, 0, t], -1))

    def gather_matrix(m, carry):
        for c in range(gys):
            value = jnp.zeros((cap, lanes), jnp.int32)
            for t in range(cap):
                value = jnp.where(slot == t, node_of(m, c, t), value)
            wanted = jnp.concatenate(
                [jnp.where(value >= 0, value * DOFS + d, -1) for d in range(DOFS)], axis=0)
            lane = lax.broadcasted_iota(jnp.int32, (rows, lanes), 1)
            for b in range(nb * width // lanes):
                hot = jnp.where(wanted == lane + b * lanes, F32(1.0), F32(0.0)).astype(BF16)
                gat[m, c * rows:(c + 1) * rows, b * lanes:(b + 1) * lanes] = hot
        return carry

    lax.fori_loop(0, members, gather_matrix, 0)


    @pl.when(jnp.logical_not(rod))
    def _():
        for c in range(gys):
            kap_copy(c, my_chunk).start()

    for r in order[4:]:
        pltpu.make_async_copy(v_hbm.at[r], acc0.at[r], v_sem.at[r]).wait()
        ext[0, r] = acc0[r].astype(BF16)

    def sleeve_wait(s, how):
        def over(mine, theirs):
            how(pltpu.make_async_remote_copy(
                src_ref=mine, dst_ref=theirs, send_sem=ss.at[s], recv_sem=sr.at[s],
                device_id=peer(0), device_id_type=MESH))

        if members == 1:
            over(own.at[s], oth.at[s])
        else:
            pl.when(rod)(lambda: over(own.at[s], oth.at[s]))
            pl.when(jnp.logical_not(rod))(lambda: over(own.at[s, 0], oth.at[s, 0]))

    def gather(s):
        def one(m, carry):
            got = jnp.dot(gat[m], ext[lax.rem(s, 2), :nb].reshape(nb * width, lanes), preferred_element_type=F32)
            own[s, m] = got.astype(BF16).reshape(gys, rows, lanes)
            return carry

        lax.fori_loop(0, members, one, 0)
        each_chunk(lambda c: sleeve_copy(s, c, my_chunk).start())

    early = width // 256 * 256

    def first_blocks(s):
        def one(r, carry):
            acc0[r] = jnp.dot(a[r, 0, :, :early], ext[lax.rem(s, 2), r, :early], preferred_element_type=F32)
            return carry

        lax.fori_loop(0, nb, one, 0, unroll=4)

    def spring_forces(s):
        sleeve_wait(s, lambda copy: copy.wait_recv())
        for m in range(members):
            force = kap[m] * (own[s, m].astype(F32) - oth[s, m].astype(F32))
            dlt[m * gys * rows:(m + 1) * gys * rows] = force.astype(BF16).reshape(gys * rows, lanes)

    def main_rows(s, half):
        now = lax.rem(s, 2)

        def one(i, carry):
            r = row_of(half * 4 + i)
            left = jnp.concatenate(
                [a[r, 0, :, early:]] + [a[r, k] for k in range(1, kb)] + [sca[r]], axis=1)
            right = jnp.concatenate(
                [ext[now, r, early:]] + [ext[now, cols[k, r]] for k in range(1, kb)] + [dlt[...]], axis=0)
            c = (acc0[r] + jnp.dot(left, right, preferred_element_type=F32)) * inv[...]
            sqacc[...] += jnp.sum((c * c).reshape(width // 8, 8, lanes), axis=0)
            ext[1 - now, r] = c.astype(BF16)
            acc0[r] = c
            return carry

        lax.fori_loop(0, 4, one, 0, unroll=2)

    def line_copy(s, device, slots):
        return pltpu.make_async_remote_copy(
            src_ref=sqa.at[s, slots], dst_ref=sqa.at[s, slots],
            send_sem=as_.at[s], recv_sem=ar.at[s],
            device_id=device, device_id_type=MESH)

    def plane_copy(s, device, slots):
        return pltpu.make_async_remote_copy(
            src_ref=sqb.at[s, slots], dst_ref=sqb.at[s, slots],
            send_sem=bs.at[s], recv_sem=br.at[s],
            device_id=device, device_id_type=MESH)

    def line_all(s):
        return line_copy(s, line_peer(1), pl.ds(0, gys - 1))

    def plane_all(s):
        return plane_copy(s, plane_peer(1), pl.ds(0, n_plane - 1))

    def squares_line(s):
        sqa[s, y] = sqacc[...]
        for i in range(1, gys):
            line_copy(s, line_peer(i), y).start()

    def squares_plane(s):
        line_all(s).wait_recv()
        total = sqa[s, 0]
        for i in range(1, gys):
            total = total + sqa[s, i]
        sqb[s, plane] = total
        for i in range(1, n_plane):
            plane_copy(s, plane_peer(i), plane).start()

    def squares_end(s):
        plane_all(s).wait_recv()
        total = sqb[s, 0]
        for p in range(1, groups * gxs):
            total = total + sqb[s, p]
        scale = jnp.sqrt(jnp.sum(total, axis=0, keepdims=True) / all_dofs + EPSILON)
        norms[pl.ds(s, 1), :] = scale
        inv[...] = 1.0 / scale

    padded = sca.shape[2]
    place = lax.broadcasted_iota(jnp.int32, (8, padded), 1)
    within = lax.rem(place, rows)
    key = lax.div(place, rows) * cap + lax.rem(within, cap)

    def slot_row(j, value):
        c = lax.div(j, cap)
        node = node_of(lax.div(c, gys), lax.rem(c, gys), lax.rem(j, cap))
        return jnp.where(key == j, node, value)

    node_row = lax.fori_loop(0, chunks * cap, slot_row, jnp.full((8, padded), -1, jnp.int32))
    node_row = jnp.where(node_row >= 0, node_row * DOFS + lax.div(within, cap), -1)

    def scatter_matrix(r, carry):
        dof = lax.broadcasted_iota(jnp.int32, (width, padded), 0) + r * width
        sca[r] = jnp.where(node_row[:1] == dof, F32(1.0), F32(0.0)).astype(BF16)
        return carry

    lax.fori_loop(0, nb, scatter_matrix, 0)
    if dlt.shape[0] > chunks * rows:
        dlt[chunks * rows:] = jnp.zeros((dlt.shape[0] - chunks * rows, lanes), BF16)
    inv[...] = jnp.ones_like(inv)
    last = MATVECS - 1

    def step(s, carry):
        gather(s)

        @pl.when(s == 0)
        def _():
            pltpu.make_async_copy(a_hbm.at[:, 0], a.at[:, 0], a0_sem).wait()

        first_blocks(s)

        @pl.when(s > 0)
        def _():
            squares_plane(s - 1)

        @pl.when((s == 0) & rod)
        def _():
            pltpu.make_async_remote_copy(
                src_ref=kap, dst_ref=kap, send_sem=ks, recv_sem=kr,
                device_id=peer(0), device_id_type=MESH).wait_recv()

        spring_forces(s)
        wait_sides(s)

        @pl.when(s > 0)
        def _():
            squares_end(s - 1)

        @pl.when(s == 0)
        def _():
            rest.wait()

        sqacc[...] = jnp.zeros_like(sqacc)

        def part(half, carry):
            main_rows(s, half)
            send_sides(s + 1, (half == 0) & (s < last))
            return carry

        lax.fori_loop(0, nb // 4, part, 0)
        squares_line(s)
        return carry

    lax.fori_loop(0, MATVECS, step, 0)
    squares_plane(last)

    def sent(s, carry):
        sleeve_wait(s, lambda copy: copy.wait_send())
        line_all(s).wait_send()
        plane_all(s).wait_send()
        return carry

    lax.fori_loop(0, MATVECS, sent, 0)

    @pl.when(jnp.logical_not(rod))
    def _():
        pltpu.make_async_remote_copy(
            src_ref=kown, dst_ref=kown, send_sem=ks, recv_sem=kr,
            device_id=peer(0), device_id_type=MESH).wait_send()

    squares_end(last)
    for r in range(nb):
        result[r] = acc0[r] * inv[...]


def local(groups, gxs, gys, start_vectors, tile_blocks, block_columns, sleeve_rod, sleeve_membrane, sleeve_stiffness):
    nb, kb, width = tile_blocks.shape[3:6]
    lanes = start_vectors.shape[5]
    cap = sleeve_rod.shape[4]
    members = groups - 1
    rows = cap * DOFS
    chunks = members * gys
    slot_rows = chunks * rows
    padded = -(-slot_rows // 256) * 256
    small = (block_columns[0, 0, 0].T, sleeve_rod[0, 0], sleeve_membrane[0], sleeve_stiffness[0])
    vmem = pl.BlockSpec(memory_space=pltpu.VMEM)
    hbm = pl.BlockSpec(memory_space=pl.ANY)
    dma = pltpu.SemaphoreType.DMA
    plane = groups * gxs
    flops = 2 * MATVECS * nb * kb * width * width * lanes
    final, norms = pl.pallas_call(
        functools.partial(kernel, groups, gxs, gys, nb, kb, width, lanes, rows),
        out_shape=(
            pltpu.VMEM((nb, width, lanes), F32),
            pltpu.VMEM((MATVECS, lanes), F32),
        ),
        in_specs=[hbm] * 6,
        out_specs=(vmem, vmem),
        scratch_shapes=[
            *[pltpu.SMEM(array.shape, array.dtype) for array in small],
            pltpu.VMEM((nb, kb, width, width), BF16),
            pltpu.VMEM((2, nb + 4, width, lanes), BF16),
            pltpu.VMEM((MATVECS, 4, width, lanes), BF16),
            pltpu.VMEM((nb, width, lanes), F32),
            pltpu.VMEM((members, gys * rows, nb * width), BF16),
            pltpu.VMEM((nb, width, padded), BF16),
            pltpu.VMEM((MATVECS, members, gys, rows, lanes), BF16),
            pltpu.VMEM((MATVECS, members, gys, rows, lanes), BF16),
            pltpu.VMEM((gys, rows, lanes), F32),
            pltpu.VMEM((members, gys, rows, lanes), F32),
            pltpu.VMEM((padded, lanes), BF16),
            pltpu.VMEM((8, lanes), F32),
            pltpu.VMEM((MATVECS, gys, 8, lanes), F32),
            pltpu.VMEM((MATVECS, plane, 8, lanes), F32),
            pltpu.VMEM((1, lanes), F32),
            dma((4,)), dma((nb,)), dma, dma,
            dma((MATVECS, 4)), dma((MATVECS, 4)),
            dma((MATVECS,)), dma((MATVECS,)),
            dma, dma,
            *[dma((MATVECS,))] * 4,
        ],
        compiler_params=pltpu.CompilerParams(
            collective_id=0, has_side_effects=True, vmem_limit_bytes=58 * 2**20),
        cost_estimate=pl.CostEstimate(flops=flops, bytes_accessed=tile_blocks.size * 2, transcendentals=0),
    )(*small,
      start_vectors.reshape(nb, width, lanes), tile_blocks.reshape(nb, kb, width, width))
    return (final[None, None, None], norms)


def solution(mesh):
    return jax.shard_map(
        functools.partial(local, mesh.shape["group"], mesh.shape["gx"], mesh.shape["gy"]),
        mesh=mesh,
        in_specs=(
            P("group", "gx", "gy", None, None, None),
            P("group", "gx", "gy", None, None, None, None),
            P("group", "gx", "gy", None, None),
            P("gx", "gy", None, None, None),
            P("gx", None, None, "gy", None),
            P("gx", None, None, "gy", None),
        ),
        out_specs=(P("group", "gx", "gy", None, None, None), P()),
        check_vma=False,
    )
```

```python
import functools

import jax
import jax.numpy as jnp
from jax import lax
from jax.experimental import pallas as pl
from jax.experimental.pallas import tpu as pltpu
from jax.sharding import PartitionSpec as P

MATVECS = 3
DOFS = 6
EPSILON = 1e-06
MESH = pl.DeviceIdType.MESH
F32 = jnp.float32
BF16 = jnp.bfloat16


def kernel(groups, gxs, gys, nb, kb, width, lanes, rows,
           cols_hbm, rod_hbm, memb_hbm, stiff_hbm, v_hbm, a_hbm,
           result, norms,
           cols, rod_nodes, memb_nodes, stiff, a, ext, land, acc0, gat, sca, own, oth, kown, kap, dlt, sqacc, sqa, sqb, inv,
           i_sem, v_sem, a0_sem, a_sem, gs, gr, ss, sr, ks, kr, as_, ar, bs, br):
    g = lax.axis_index("group")
    x = lax.axis_index("gx")
    y = lax.axis_index("gy")
    plane = g * gxs + x
    rod = g == 0
    members = groups - 1
    chunks = members * gys
    all_dofs = float(groups * gxs * gys * nb * width)

    def row_of(i):
        half, odd = lax.div(i, 2), lax.rem(i, 2)
        return half * (1 - 2 * odd) + odd * (nb - 1)

    order = [i // 2 if i % 2 == 0 else nb - 1 - i // 2 for i in range(nb)]
    for r in order:
        pltpu.make_async_copy(v_hbm.at[r], acc0.at[r], v_sem.at[r]).start()
    pltpu.make_async_copy(a_hbm.at[:, 0], a.at[:, 0], a0_sem).start()
    rest = pltpu.make_async_copy(a_hbm.at[:, pl.ds(1, kb - 1)], a.at[:, pl.ds(1, kb - 1)], a_sem)
    rest.start()

    small = [
        pltpu.make_async_copy(src, dst, i_sem.at[i])
        for i, (src, dst) in enumerate(
            ((rod_hbm, rod_nodes), (memb_hbm, memb_nodes), (stiff_hbm, stiff), (cols_hbm, cols)))
    ]
    for copy in small:
        copy.start()

    barrier = pltpu.get_barrier_semaphore()
    n_plane = groups * gxs

    def line_peer(i):
        return (g, x, lax.rem(y + i, gys))

    def plane_peer(i):
        p = lax.rem(plane + i, n_plane)
        return (lax.div(p, gxs), lax.rem(p, gxs), y)

    for i in range(1, gys):
        pl.semaphore_signal(barrier, inc=1, device_id=line_peer(i), device_id_type=MESH)
    for i in range(1, n_plane):
        pl.semaphore_signal(barrier, inc=1, device_id=plane_peer(i), device_id_type=MESH)

    def peer(c):
        return (1 - g if members == 1 else jnp.where(rod, c // gys + 1, 0), x, c % gys)

    def each_chunk(body):
        for c in range(chunks):
            if c < gys:
                body(c)
            else:
                pl.when(rod)(functools.partial(body, c))

    each_chunk(lambda c: pl.semaphore_signal(barrier, inc=1, device_id=peer(c), device_id_type=MESH))

    sides = (
        (nb - 1, x < gxs - 1, lambda: (g, x + 1, y), x > 0, lambda: (g, x - 1, y)),
        (0, x > 0, lambda: (g, x - 1, y), x < gxs - 1, lambda: (g, x + 1, y)),
        (1, y < gys - 1, lambda: (g, x, y + 1), y > 0, lambda: (g, x, y - 1)),
        (nb - 2, y > 0, lambda: (g, x, y - 1), y < gys - 1, lambda: (g, x, y + 1)),
    )
    for r in order[:4]:
        pltpu.make_async_copy(v_hbm.at[r], acc0.at[r], v_sem.at[r]).wait()
        ext[0, r] = acc0[r].astype(BF16)

    pl.semaphore_wait(barrier, gys - 1 + groups * gxs - 1 + jnp.where(rod, chunks, gys))

    def side_copy(s, d, device):
        return pltpu.make_async_remote_copy(
            src_ref=ext.at[lax.rem(s, 2), sides[d][0]], dst_ref=land.at[s, d],
            send_sem=gs.at[s, d], recv_sem=gr.at[s, d],
            device_id=device, device_id_type=MESH)

    def send_sides(s, more=True):
        for d, (_, sends, to, _, _) in enumerate(sides):
            @pl.when(sends & more)
            def _():
                side_copy(s, d, to()).start()

    def wait_sides(s):
        for d, (_, _, _, hears, source) in enumerate(sides):
            @pl.when(hears)
            def _():
                side_copy(s, d, source()).wait_recv()
        for d, (_, sends, to, _, _) in enumerate(sides):
            ext[lax.rem(s, 2), nb + d] = land[s, d]

            @pl.when(sends)
            def _():
                side_copy(s, d, to()).wait_send()

    my_chunk = jnp.where(rod, y, (g - 1) * gys + y)

    def sleeve_copy(s, c, dst):
        return pltpu.make_async_remote_copy(
            src_ref=own.at[s, c // gys, c % gys], dst_ref=oth.at[s, dst // gys, dst % gys],
            send_sem=ss.at[s], recv_sem=sr.at[s],
            device_id=peer(c), device_id_type=MESH)

    def kap_copy(c, dst):
        return pltpu.make_async_remote_copy(
            src_ref=kown.at[c % gys], dst_ref=kap.at[dst // gys, dst % gys],
            send_sem=ks, recv_sem=kr,
            device_id=peer(c), device_id_type=MESH)

    send_sides(0)
    for copy in small:
        copy.wait()

    for d, (_, _, _, hears, _) in enumerate(sides):
        @pl.when(jnp.logical_not(hears))
        def _():
            for s in range(MATVECS):
                land[s, d] = jnp.zeros((width, lanes), BF16)

    cap = rows // DOFS
    member = jnp.maximum(g - 1, 0)
    slot = lax.broadcasted_iota(jnp.int32, (cap, lanes), 0)
    for c in range(gys):
        value = jnp.zeros((cap, lanes), F32)
        for t in range(cap):
            value = jnp.where(slot == t, stiff[c, member, 0, t], value)
        for d in range(DOFS):
            kown[c, d * cap:(d + 1) * cap] = value

    @pl.when(jnp.logical_not(rod))
    def _():
        kap[0] = kown[...]
        for m in range(1, members):
            kap[m] = jnp.zeros((gys, rows, lanes), F32)
            for s in range(MATVECS):
                oth[s, m] = jnp.zeros((gys, rows, lanes), BF16)

    def node_of(m, c, t):
        return jnp.where(rod, rod_nodes[m, c, t], jnp.where(m == 0, memb_nodes[c, member, 0, t], -1))

    def gather_matrix(m, carry):
        for c in range(gys):
            value = jnp.zeros((cap, lanes), jnp.int32)
            for t in range(cap):
                value = jnp.where(slot == t, node_of(m, c, t), value)
            wanted = jnp.concatenate(
                [jnp.where(value >= 0, value * DOFS + d, -1) for d in range(DOFS)], axis=0)
            lane = lax.broadcasted_iota(jnp.int32, (rows, lanes), 1)
            for b in range(nb * width // lanes):
                hot = jnp.where(wanted == lane + b * lanes, F32(1.0), F32(0.0)).astype(BF16)
                gat[m, c * rows:(c + 1) * rows, b * lanes:(b + 1) * lanes] = hot
        return carry

    lax.fori_loop(0, members, gather_matrix, 0)


    @pl.when(jnp.logical_not(rod))
    def _():
        for c in range(gys):
            kap_copy(c, my_chunk).start()

    for r in order[4:]:
        pltpu.make_async_copy(v_hbm.at[r], acc0.at[r], v_sem.at[r]).wait()
        ext[0, r] = acc0[r].astype(BF16)

    def sleeve_wait(s, how):
        def over(mine, theirs):
            how(pltpu.make_async_remote_copy(
                src_ref=mine, dst_ref=theirs, send_sem=ss.at[s], recv_sem=sr.at[s],
                device_id=peer(0), device_id_type=MESH))

        if members == 1:
            over(own.at[s], oth.at[s])
        else:
            pl.when(rod)(lambda: over(own.at[s], oth.at[s]))
            pl.when(jnp.logical_not(rod))(lambda: over(own.at[s, 0], oth.at[s, 0]))

    def gather(s):
        def one(m, carry):
            got = jnp.dot(gat[m], ext[lax.rem(s, 2), :nb].reshape(nb * width, lanes), preferred_element_type=F32)
            own[s, m] = got.astype(BF16).reshape(gys, rows, lanes)
            return carry

        lax.fori_loop(0, members, one, 0)
        each_chunk(lambda c: sleeve_copy(s, c, my_chunk).start())

    early = width // 256 * 256

    def first_blocks(s):
        def one(r, carry):
            acc0[r] = jnp.dot(a[r, 0, :, :early], ext[lax.rem(s, 2), r, :early], preferred_element_type=F32)
            return carry

        lax.fori_loop(0, nb, one, 0, unroll=4)

    def spring_forces(s):
        sleeve_wait(s, lambda copy: copy.wait_recv())
        for m in range(members):
            force = kap[m] * (own[s, m].astype(F32) - oth[s, m].astype(F32))
            dlt[m * gys * rows:(m + 1) * gys * rows] = force.astype(BF16).reshape(gys * rows, lanes)

    def main_rows(s, half):
        now = lax.rem(s, 2)

        def one(i, carry):
            r = row_of(half * 4 + i)
            c = acc0[r] + jnp.dot(a[r, 0, :, early:], ext[now, r, early:], preferred_element_type=F32)
            for k in range(1, kb):
                c = c + jnp.dot(a[r, k], ext[now, cols[k, r]], preferred_element_type=F32)
            c = (c + jnp.dot(sca[r], dlt[...], preferred_element_type=F32)) * inv[...]
            sqacc[...] += jnp.sum((c * c).reshape(width // 8, 8, lanes), axis=0)
            ext[1 - now, r] = c.astype(BF16)
            acc0[r] = c
            return carry

        lax.fori_loop(0, 4, one, 0, unroll=2)

    def line_copy(s, device, slots):
        return pltpu.make_async_remote_copy(
            src_ref=sqa.at[s, slots], dst_ref=sqa.at[s, slots],
            send_sem=as_.at[s], recv_sem=ar.at[s],
            device_id=device, device_id_type=MESH)

    def plane_copy(s, device, slots):
        return pltpu.make_async_remote_copy(
            src_ref=sqb.at[s, slots], dst_ref=sqb.at[s, slots],
            send_sem=bs.at[s], recv_sem=br.at[s],
            device_id=device, device_id_type=MESH)

    def line_all(s):
        return line_copy(s, line_peer(1), pl.ds(0, gys - 1))

    def plane_all(s):
        return plane_copy(s, plane_peer(1), pl.ds(0, n_plane - 1))

    def squares_line(s):
        sqa[s, y] = sqacc[...]
        for i in range(1, gys):
            line_copy(s, line_peer(i), y).start()

    def squares_plane(s):
        line_all(s).wait_recv()
        total = sqa[s, 0]
        for i in range(1, gys):
            total = total + sqa[s, i]
        sqb[s, plane] = total
        for i in range(1, n_plane):
            plane_copy(s, plane_peer(i), plane).start()

    def squares_end(s):
        plane_all(s).wait_recv()
        total = sqb[s, 0]
        for p in range(1, groups * gxs):
            total = total + sqb[s, p]
        scale = jnp.sqrt(jnp.sum(total, axis=0, keepdims=True) / all_dofs + EPSILON)
        norms[pl.ds(s, 1), :] = scale
        inv[...] = 1.0 / scale

    padded = sca.shape[2]
    place = lax.broadcasted_iota(jnp.int32, (8, padded), 1)
    within = lax.rem(place, rows)
    key = lax.div(place, rows) * cap + lax.rem(within, cap)

    def slot_row(j, value):
        c = lax.div(j, cap)
        node = node_of(lax.div(c, gys), lax.rem(c, gys), lax.rem(j, cap))
        return jnp.where(key == j, node, value)

    node_row = lax.fori_loop(0, chunks * cap, slot_row, jnp.full((8, padded), -1, jnp.int32))
    node_row = jnp.where(node_row >= 0, node_row * DOFS + lax.div(within, cap), -1)

    def scatter_matrix(r, carry):
        dof = lax.broadcasted_iota(jnp.int32, (width, padded), 0) + r * width
        sca[r] = jnp.where(node_row[:1] == dof, F32(1.0), F32(0.0)).astype(BF16)
        return carry

    lax.fori_loop(0, nb, scatter_matrix, 0)
    if dlt.shape[0] > chunks * rows:
        dlt[chunks * rows:] = jnp.zeros((dlt.shape[0] - chunks * rows, lanes), BF16)
    inv[...] = jnp.ones_like(inv)
    last = MATVECS - 1

    def step(s, carry):
        gather(s)

        @pl.when(s == 0)
        def _():
            pltpu.make_async_copy(a_hbm.at[:, 0], a.at[:, 0], a0_sem).wait()

        first_blocks(s)

        @pl.when(s > 0)
        def _():
            squares_plane(s - 1)

        @pl.when((s == 0) & rod)
        def _():
            pltpu.make_async_remote_copy(
                src_ref=kap, dst_ref=kap, send_sem=ks, recv_sem=kr,
                device_id=peer(0), device_id_type=MESH).wait_recv()

        spring_forces(s)
        wait_sides(s)

        @pl.when(s > 0)
        def _():
            squares_end(s - 1)

        @pl.when(s == 0)
        def _():
            rest.wait()

        sqacc[...] = jnp.zeros_like(sqacc)

        def part(half, carry):
            main_rows(s, half)
            send_sides(s + 1, (half == 0) & (s < last))
            return carry

        lax.fori_loop(0, nb // 4, part, 0)
        squares_line(s)
        return carry

    lax.fori_loop(0, MATVECS, step, 0)
    squares_plane(last)

    def sent(s, carry):
        sleeve_wait(s, lambda copy: copy.wait_send())
        line_all(s).wait_send()
        plane_all(s).wait_send()
        return carry

    lax.fori_loop(0, MATVECS, sent, 0)

    @pl.when(jnp.logical_not(rod))
    def _():
        pltpu.make_async_remote_copy(
            src_ref=kown, dst_ref=kown, send_sem=ks, recv_sem=kr,
            device_id=peer(0), device_id_type=MESH).wait_send()

    squares_end(last)
    for r in range(nb):
        result[r] = acc0[r] * inv[...]


def local(groups, gxs, gys, start_vectors, tile_blocks, block_columns, sleeve_rod, sleeve_membrane, sleeve_stiffness):
    nb, kb, width = tile_blocks.shape[3:6]
    lanes = start_vectors.shape[5]
    cap = sleeve_rod.shape[4]
    members = groups - 1
    rows = cap * DOFS
    chunks = members * gys
    slot_rows = chunks * rows
    padded = -(-slot_rows // 256) * 256
    small = (block_columns[0, 0, 0].T, sleeve_rod[0, 0], sleeve_membrane[0], sleeve_stiffness[0])
    vmem = pl.BlockSpec(memory_space=pltpu.VMEM)
    hbm = pl.BlockSpec(memory_space=pl.ANY)
    dma = pltpu.SemaphoreType.DMA
    plane = groups * gxs
    flops = 2 * MATVECS * nb * kb * width * width * lanes
    final, norms = pl.pallas_call(
        functools.partial(kernel, groups, gxs, gys, nb, kb, width, lanes, rows),
        out_shape=(
            pltpu.VMEM((nb, width, lanes), F32),
            pltpu.VMEM((MATVECS, lanes), F32),
        ),
        in_specs=[hbm] * 6,
        out_specs=(vmem, vmem),
        scratch_shapes=[
            *[pltpu.SMEM(array.shape, array.dtype) for array in small],
            pltpu.VMEM((nb, kb, width, width), BF16),
            pltpu.VMEM((2, nb + 4, width, lanes), BF16),
            pltpu.VMEM((MATVECS, 4, width, lanes), BF16),
            pltpu.VMEM((nb, width, lanes), F32),
            pltpu.VMEM((members, gys * rows, nb * width), BF16),
            pltpu.VMEM((nb, width, padded), BF16),
            pltpu.VMEM((MATVECS, members, gys, rows, lanes), BF16),
            pltpu.VMEM((MATVECS, members, gys, rows, lanes), BF16),
            pltpu.VMEM((gys, rows, lanes), F32),
            pltpu.VMEM((members, gys, rows, lanes), F32),
            pltpu.VMEM((padded, lanes), BF16),
            pltpu.VMEM((8, lanes), F32),
            pltpu.VMEM((MATVECS, gys, 8, lanes), F32),
            pltpu.VMEM((MATVECS, plane, 8, lanes), F32),
            pltpu.VMEM((1, lanes), F32),
            dma((4,)), dma((nb,)), dma, dma,
            dma((MATVECS, 4)), dma((MATVECS, 4)),
            dma((MATVECS,)), dma((MATVECS,)),
            dma, dma,
            *[dma((MATVECS,))] * 4,
        ],
        compiler_params=pltpu.CompilerParams(
            collective_id=0, has_side_effects=True, vmem_limit_bytes=58 * 2**20),
        cost_estimate=pl.CostEstimate(flops=flops, bytes_accessed=tile_blocks.size * 2, transcendentals=0),
    )(*small,
      start_vectors.reshape(nb, width, lanes), tile_blocks.reshape(nb, kb, width, width))
    return (final[None, None, None], norms)


def solution(mesh):
    return jax.shard_map(
        functools.partial(local, mesh.shape["group"], mesh.shape["gx"], mesh.shape["gy"]),
        mesh=mesh,
        in_specs=(
            P("group", "gx", "gy", None, None, None),
            P("group", "gx", "gy", None, None, None, None),
            P("group", "gx", "gy", None, None),
            P("gx", "gy", None, None, None),
            P("gx", None, None, "gy", None),
            P("gx", None, None, "gy", None),
        ),
        out_specs=(P("group", "gx", "gy", None, None, None), P()),
        check_vma=False,
    )
```
